32 devices in a mesh: dp: 4 (over y, x), mp: 8 (over z, core).
Axes of the slice: x: 2, y: 2, z: 4, core: 2. Of those that a mesh axis runs over, the one named last changes fastest.
Arguments:
- inputs: bfloat16 [128, 10240], P('dp', 'mp'), may hold values from -6 to 6
- out_grads: bfloat16 [128, 10240], P('dp', 'mp'), may hold values from -6 to 6
- w_in: bfloat16 [10240, 18432], P('mp', 'dp'), may hold values from -0.0625 to 0.0625
- w_out: bfloat16 [18432, 10240], P('dp', 'mp'), may hold values from -0.046875 to 0.046875
Outputs:
- in_grads: float32 [128, 10240], P('dp', 'mp')
- grad_w_in: bfloat16 [10240, 18432], P('mp', 'dp')
- grad_w_out: bfloat16 [18432, 10240], P('dp', 'mp')
The draws below stay inside these ranges and needn't reach their ends.
All inputs are finite; a program needn't handle non-finite values.
Results may differ from the reference program's by a relative error of at most 0.005.
Values may be sent and summed in bfloat16 or wider, within the bound.
No kernel may reach another device: no remote copies, remote signals or barrier semaphores. Data moves between devices by JAX's collectives and lax.ppermute only.
A program may use at most 128 MiB of HBM per device.

```python
import math
import jax
import jax.numpy as jnp

D = 10240
FF = 18432
TOKENS = 128


def levels(key, extent, split, least, top_value):
    gain = 1.0
    for axis_at, parts in split:
        draws = jax.random.uniform(jax.random.fold_in(jax.random.fold_in(key, 6), axis_at), (parts,), jnp.float32, least / len(split), top_value / len(split))
        gain = gain * jnp.repeat(jnp.exp(draws), extent[axis_at] // parts).reshape((-1,) + (1,) * (len(extent) - 1 - axis_at))
    return gain


def noise(rng, extent, width, limit, shards=(), kind=jnp.bfloat16):
    drawn = width * jax.random.normal(rng, extent, jnp.float32)
    if shards:
        drawn = drawn * levels(rng, extent, shards, -0.22, 0.18)
    return jnp.clip(drawn, -limit, limit).astype(kind)


def setup_inputs(seed: int = 0) -> dict:
    key_of = jax.random.split(jax.random.key(seed), 5)
    return {
        "inputs": noise(key_of[0], (TOKENS, D), 1.0, 6.0, ((0, 4), (1, 8))),
        "out_grads": noise(key_of[1], (TOKENS, D), 1.0, 6.0, ((0, 4), (1, 8))),
        "w_in": noise(key_of[2], (D, FF), D ** -0.5, 0.0625, ((0, 8), (1, 4))),
        "w_out": noise(key_of[3], (FF, D), FF ** -0.5, 0.046875, ((0, 4), (1, 8))),
    }


def gelu_parts(preact):
    cumul = 0.5 * (1.0 + jax.scipy.special.erf(preact * (1.0 / math.sqrt(2.0))))
    density = jnp.exp(-0.5 * preact * preact) * (1.0 / math.sqrt(2.0 * math.pi))
    return (preact * cumul, cumul + preact * density)

def reference(inputs, out_grads, w_in, w_out):
    preact = jnp.dot(inputs, w_in, preferred_element_type=jnp.float32)
    grad_act = jnp.dot(out_grads, w_out.T, preferred_element_type=jnp.float32)
    gelu_value, gelu_slope = gelu_parts(preact)
    activation = gelu_value.astype(jnp.bfloat16)
    grad_preact = (grad_act * gelu_slope).astype(jnp.bfloat16)
    in_grads = jnp.dot(grad_preact, w_in.T, preferred_element_type=jnp.float32)
    factor = 1.0 / math.sqrt(TOKENS)
    grad_w_in = (jnp.dot(inputs.T, grad_preact, preferred_element_type=jnp.float32) * factor).astype(jnp.bfloat16)
    grad_w_out = (jnp.dot(activation.T, out_grads, preferred_element_type=jnp.float32) * factor).astype(jnp.bfloat16)
    return (in_grads, grad_w_in, grad_w_out)
```

```python
import functools
import math

import jax
import jax.numpy as jnp
from jax import lax
from jax.experimental import pallas as pl
from jax.experimental.pallas import tpu as pltpu
from jax.sharding import PartitionSpec as P

BF16 = jnp.bfloat16
F32 = jnp.float32
CHUNKS = 2
BLOCK = 768
VMEM_BYTES = 40 * 1024 * 1024


def gelu_parts(preact):
    cumul = 0.5 * (1.0 + jax.scipy.special.erf(preact * (1.0 / math.sqrt(2.0))))
    density = jnp.exp(-0.5 * preact * preact) * (1.0 / math.sqrt(2.0 * math.pi))
    return (preact * cumul, cumul + preact * density)


def contract(left, right, left_dim, right_dim):
    return lax.dot_general(
        left,
        right,
        (((left_dim,), (right_dim,)), ((), ())),
        preferred_element_type=F32,
    )


def bit_reversed(count):
    bits = count.bit_length() - 1
    return [
        sum(((slot >> bit) & 1) << (bits - 1 - bit) for bit in range(bits))
        for slot in range(count)
    ]


def exchange(array, axis, size, step):
    return lax.ppermute(array, axis, [(i, i ^ step) for i in range(size)])


def whole(*shape):
    return pl.BlockSpec(shape, lambda step: (0,) * len(shape))


def params():
    return pltpu.CompilerParams(vmem_limit_bytes=VMEM_BYTES)


def cost(flops, size):
    return pl.CostEstimate(flops=flops, bytes_accessed=size, transcendentals=0)


def slot_matrix(rank, total, slots):
    piece = total // slots
    blocks = jnp.array(bit_reversed(slots), jnp.int32) ^ rank
    source = (blocks[:, None] * piece + jnp.arange(piece, dtype=jnp.int32)).reshape(-1)
    return (source[:, None] == jnp.arange(total, dtype=jnp.int32)).astype(BF16)


def forward(xs, gs, w_in, w_out, start, width):
    total, features = xs.shape
    half = total // 2
    first, steps = start // BLOCK, width // BLOCK

    def kernel(xs_ref, gs_ref, wi_ref, wo_ref, keep_ref, send_ref):
        pre = contract(xs_ref[...], wi_ref[...], 1, 0)
        grad = contract(gs_ref[...], wo_ref[...], 1, 1)
        keep_ref[0] = pre[:half]
        keep_ref[1] = grad[:half]
        send_ref[0] = pre[half:].astype(BF16)
        send_ref[1] = grad[half:].astype(BF16)

    return pl.pallas_call(
        kernel,
        grid=(steps,),
        out_shape=(
            jax.ShapeDtypeStruct((2, half, width), F32),
            jax.ShapeDtypeStruct((2, half, width), BF16),
        ),
        in_specs=[
            pl.BlockSpec((total, features), lambda i: (0, 0)),
            pl.BlockSpec((total, features), lambda i: (0, 0)),
            pl.BlockSpec((features, BLOCK), lambda i: (0, first + i)),
            pl.BlockSpec((BLOCK, features), lambda i: (first + i, 0)),
        ],
        out_specs=(
            pl.BlockSpec((2, half, BLOCK), lambda i: (0, 0, i)),
            pl.BlockSpec((2, half, BLOCK), lambda i: (0, 0, i)),
        ),
        compiler_params=params(),
        cost_estimate=cost(4 * total * features * width, 4 * features * width),
        name="forward",
    )(xs, gs, w_in, w_out)


def input_grads(lower, upper, order, w_in, carried, start, width):
    half = lower.shape[1]
    features = w_in.shape[0]
    first, steps = start // BLOCK, width // BLOCK

    def kernel(*refs):
        low_ref, up_ref, order_ref, wi_ref = refs[:4]
        out_ref = refs[-1]
        step = pl.program_id(0)
        grad = jnp.concatenate([low_ref[0], up_ref[0]], axis=0)
        grad = contract(order_ref[...], grad, 1, 0).astype(BF16)
        value = contract(grad, wi_ref[...], 1, 1)

        @pl.when(step == 0)
        def _():
            out_ref[...] = value if carried is None else refs[4][...] + value

        @pl.when(step > 0)
        def _():
            out_ref[...] += value

    block = pl.BlockSpec((1, half, BLOCK), lambda i: (1, 0, i))
    return pl.pallas_call(
        kernel,
        grid=(steps,),
        out_shape=jax.ShapeDtypeStruct((2 * half, features), F32),
        in_specs=[
            block,
            block,
            whole(2 * half, 2 * half),
            pl.BlockSpec((features, BLOCK), lambda i: (0, first + i)),
        ]
        + ([] if carried is None else [whole(2 * half, features)]),
        out_specs=whole(2 * half, features),
        compiler_params=params(),
        cost_estimate=cost(4 * half * features * width, 2 * features * width),
        name="input_grads",
    )(lower, upper, order, w_in, *([] if carried is None else [carried]))


def weight_grads(xt, gs, finals, hidden, factor):
    features, total = xt.shape
    half = total // 2
    chunks = len(finals)
    steps = hidden // chunks // BLOCK

    def kernel(xt_ref, gs_ref, *refs):
        in_ref, out_ref = refs[-2:]
        step = pl.program_id(0)

        def work(la_ref, ua_ref, lg_ref, ug_ref):
            act = jnp.concatenate([la_ref[0], ua_ref[0]], axis=0)
            grad = jnp.concatenate([lg_ref[0], ug_ref[0]], axis=0)
            turned = act.astype(F32).T.astype(BF16)
            in_ref[...] = (contract(xt_ref[...], grad, 1, 0) * factor).astype(BF16)
            out_ref[...] = (contract(turned, gs_ref[...], 1, 0) * factor).astype(BF16)

        for chunk in range(chunks):
            here = (step >= chunk * steps) & (step < (chunk + 1) * steps)
            pl.when(here)(functools.partial(work, *refs[4 * chunk : 4 * chunk + 4]))

    def block(chunk, which):
        def place(i):
            return which, 0, jnp.clip(i - chunk * steps, 0, steps - 1)

        return pl.BlockSpec((1, half, BLOCK), place)

    specs, operands = [], []
    for chunk, (lower, upper) in enumerate(finals):
        specs += [block(chunk, 0), block(chunk, 0), block(chunk, 1), block(chunk, 1)]
        operands += [lower, upper, lower, upper]
    return pl.pallas_call(
        kernel,
        grid=(chunks * steps,),
        out_shape=(
            jax.ShapeDtypeStruct((features, hidden), BF16),
            jax.ShapeDtypeStruct((hidden, features), BF16),
        ),
        in_specs=[whole(features, total), whole(total, features)] + specs,
        out_specs=(
            pl.BlockSpec((features, BLOCK), lambda i: (0, i)),
            pl.BlockSpec((BLOCK, features), lambda i: (i, 0)),
        ),
        compiler_params=params(),
        cost_estimate=cost(4 * total * features * hidden, 4 * features * hidden),
        name="weight_grads",
    )(xt, gs, *operands)


def halve(keep, received):
    half, width = keep.shape[1] // 2, keep.shape[2]

    def kernel(keep_ref, received_ref, next_ref, send_ref):
        next_ref[...] = keep_ref[:, :half] + received_ref[:, :half].astype(F32)
        send_ref[...] = (keep_ref[:, half:] + received_ref[:, half:].astype(F32)).astype(BF16)

    return pl.pallas_call(
        kernel,
        out_shape=(
            jax.ShapeDtypeStruct((2, half, width), F32),
            jax.ShapeDtypeStruct((2, half, width), BF16),
        ),
        grid=(1,),
        in_specs=[whole(2, 2 * half, width)] * 2,
        out_specs=(whole(2, half, width),) * 2,
        compiler_params=params(),
        cost_estimate=cost(4 * half * width, 24 * half * width),
        name="halve",
    )(keep, received)


def activate(keep, received):
    def kernel(keep_ref, received_ref, out_ref):
        value, slope = gelu_parts(keep_ref[0] + received_ref[0].astype(F32))
        grad = keep_ref[1] + received_ref[1].astype(F32)
        out_ref[0] = value.astype(BF16)
        out_ref[1] = (grad * slope).astype(BF16)

    return pl.pallas_call(
        kernel,
        out_shape=jax.ShapeDtypeStruct(keep.shape, BF16),
        grid=(1,),
        in_specs=[whole(*keep.shape)] * 2,
        out_specs=whole(*keep.shape),
        compiler_params=params(),
        cost_estimate=cost(20 * keep.size, 8 * keep.size),
        name="activate",
    )(keep, received)


def scatter_sum(keep, send, size):
    step = 1
    while 2 * step < size:
        keep, send = halve(keep, exchange(send, "mp", size, step))
        step *= 2
    return activate(keep, exchange(send, "mp", size, step))


def gather_rows(own, size):
    step = size // 2
    while step > 1:
        own = jnp.concatenate([own, exchange(own, "mp", size, step)], axis=1)
        step //= 2
    return own, exchange(own, "mp", size, 1)


def local(inputs, out_grads, w_in, w_out, dp, mp):
    hidden = w_in.shape[1]
    width = hidden // CHUNKS
    rows = inputs.shape[0]
    factor = 1.0 / math.sqrt(rows * dp)
    order = slot_matrix(lax.axis_index("mp").astype(jnp.int32), rows * dp, mp)

    def gather_tokens(own):
        return jnp.concatenate([own] + [exchange(own, "dp", dp, j) for j in range(1, dp)])

    gathered_x, gathered_g = gather_tokens(inputs), gather_tokens(out_grads)
    xs = contract(order, gathered_x, 1, 0).astype(BF16)
    gs = contract(order, gathered_g, 1, 0).astype(BF16)
    xt = contract(gathered_x, order, 0, 1).astype(BF16)

    finals = []
    for chunk in range(CHUNKS):
        keep, send = forward(xs, gs, w_in, w_out, chunk * width, width)
        finals.append(gather_rows(scatter_sum(keep, send, mp), mp))

    partial = None
    for chunk, (lower, upper) in enumerate(finals):
        partial = input_grads(lower, upper, order.T, w_in, partial, chunk * width, width)
    in_total = partial[:rows]
    for j in range(1, dp):
        part = partial[j * rows : (j + 1) * rows].astype(BF16)
        in_total = in_total + exchange(part, "dp", dp, j).astype(F32)
    return (in_total, *weight_grads(xt, gs, finals, hidden, factor))


def solution(mesh):
    sizes = dict(mesh.shape)
    return jax.shard_map(
        functools.partial(local, dp=sizes["dp"], mp=sizes["mp"]),
        mesh=mesh,
        in_specs=(P("dp", "mp"), P("dp", "mp"), P("mp", "dp"), P("dp", "mp")),
        out_specs=(P("dp", "mp"), P("mp", "dp"), P("dp", "mp")),
        check_vma=False,
    )
```

```python
import functools
import math

import jax
import jax.numpy as jnp
from jax import lax
from jax.experimental import pallas as pl
from jax.experimental.pallas import tpu as pltpu
from jax.sharding import PartitionSpec as P

BF16 = jnp.bfloat16
F32 = jnp.float32
GROUPS = 3
BLOCK = 512
VMEM_BYTES = 48 * 1024 * 1024
SMALL_BYTES = 16 * 1024 * 1024
SCALAR = pl.BlockSpec(memory_space=pltpu.SMEM)


def gelu_parts(preact):
    cumul = 0.5 * (1.0 + jax.scipy.special.erf(preact * (1.0 / math.sqrt(2.0))))
    density = jnp.exp(-0.5 * preact * preact) * (1.0 / math.sqrt(2.0 * math.pi))
    return (preact * cumul, cumul + preact * density)


def contract(left, right, left_dim, right_dim):
    return lax.dot_general(
        left,
        right,
        (((left_dim,), (right_dim,)), ((), ())),
        preferred_element_type=F32,
    )


def exchange(array, axis, size, step):
    return lax.ppermute(array, axis, [(i, i ^ step) for i in range(size)])


def whole(*shape):
    return pl.BlockSpec(shape, lambda step: (0,) * len(shape))


def params(size=VMEM_BYTES):
    return pltpu.CompilerParams(vmem_limit_bytes=size)


def cost(flops, size):
    return pl.CostEstimate(flops=flops, bytes_accessed=size, transcendentals=0)


def by_bit(rank_ref, bit, choose):
    side = (rank_ref[0] >> bit) & 1
    for value in range(2):
        pl.when(side == value)(functools.partial(choose, value))


def forward(rank, tokens, w_in, w_out, start, width):
    parts = len(tokens)
    rows, features = tokens[0].shape[1:]
    total = parts * rows
    half = total // 2
    first, steps = start // BLOCK, width // BLOCK

    def kernel(rank_ref, *refs):
        token_refs = refs[:parts]
        wi_ref, wo_ref, keep_ref, send_ref = refs[parts:]

        def rows_of(which):
            return jnp.concatenate([ref[which] for ref in token_refs], axis=0)

        sums = (
            contract(rows_of(0), wi_ref[...], 1, 0),
            contract(rows_of(1), wo_ref[...], 1, 1),
        )

        def choose(core):
            for which, value in enumerate(sums):
                halves = value[:half], value[half:]
                keep_ref[which] = halves[core]
                send_ref[which] = halves[1 - core].astype(BF16)

        by_bit(rank_ref, 0, choose)

    block = pl.BlockSpec((2, half, BLOCK), lambda i: (0, 0, i))
    return pl.pallas_call(
        kernel,
        grid=(steps,),
        out_shape=(
            jax.ShapeDtypeStruct((2, half, width), F32),
            jax.ShapeDtypeStruct((2, half, width), BF16),
        ),
        in_specs=[SCALAR]
        + [whole(2, rows, features)] * parts
        + [
            pl.BlockSpec((features, BLOCK), lambda i: (0, first + i)),
            pl.BlockSpec((BLOCK, features), lambda i: (first + i, 0)),
        ],
        out_specs=(block, block),
        compiler_params=params(),
        cost_estimate=cost(4 * total * features * width, 4 * features * width),
        name="forward",
    )(rank, *tokens, w_in, w_out)


def halve(rank, keep, received, bit):
    _, rows, width = keep.shape
    half = width // 2

    def kernel(rank_ref, keep_ref, received_ref, next_ref, send_ref):
        def choose(side):
            mine = slice(side * half, (side + 1) * half)
            other = slice((1 - side) * half, (2 - side) * half)
            next_ref[...] = keep_ref[:, :, mine] + received_ref[:, :, mine].astype(F32)
            send_ref[...] = (
                keep_ref[:, :, other] + received_ref[:, :, other].astype(F32)
            ).astype(BF16)

        by_bit(rank_ref, bit, choose)

    return pl.pallas_call(
        kernel,
        grid=(1,),
        out_shape=(
            jax.ShapeDtypeStruct((2, rows, half), F32),
            jax.ShapeDtypeStruct((2, rows, half), BF16),
        ),
        in_specs=[SCALAR] + [whole(2, rows, width)] * 2,
        out_specs=(whole(2, rows, half),) * 2,
        compiler_params=params(SMALL_BYTES),
        cost_estimate=cost(2 * rows * width, 12 * rows * width),
        name="halve",
    )(rank, keep, received)


def activate(keep, received):
    def kernel(keep_ref, received_ref, out_ref):
        value, slope = gelu_parts(keep_ref[0] + received_ref[0].astype(F32))
        grad = keep_ref[1] + received_ref[1].astype(F32)
        out_ref[0] = value.astype(BF16)
        out_ref[1] = (grad * slope).astype(BF16)

    return pl.pallas_call(
        kernel,
        grid=(1,),
        out_shape=jax.ShapeDtypeStruct(keep.shape, BF16),
        in_specs=[whole(*keep.shape)] * 2,
        out_specs=whole(*keep.shape),
        compiler_params=params(SMALL_BYTES),
        cost_estimate=cost(20 * keep.size, 8 * keep.size),
        name="activate",
    )(keep, received)


def join(rank, own, received, bit, axis):
    shape = list(own.shape)
    half = shape[axis]
    shape[axis] = 2 * half

    def kernel(rank_ref, own_ref, received_ref, out_ref):
        def choose(side):
            for place, source in ((side, own_ref), (1 - side, received_ref)):
                at = [slice(None)] * 3
                at[axis] = slice(place * half, (place + 1) * half)
                out_ref[tuple(at)] = source[...]

        by_bit(rank_ref, bit, choose)

    return pl.pallas_call(
        kernel,
        grid=(1,),
        out_shape=jax.ShapeDtypeStruct(shape, BF16),
        in_specs=[SCALAR] + [whole(*own.shape)] * 2,
        out_specs=whole(*shape),
        compiler_params=params(SMALL_BYTES),
        cost_estimate=cost(0, 8 * own.size),
        name="join",
    )(rank, own, received)


def reduce_and_activate(rank, keep, send, mp):
    bits = mp.bit_length() - 1
    for bit in range(1, bits):
        keep, send = halve(rank, keep, exchange(send, "mp", mp, 1 << (bit - 1)), bit)
    own = activate(keep, exchange(send, "mp", mp, 1 << (bits - 1)))
    for bit in range(bits - 1, -1, -1):
        own = join(rank, own, exchange(own, "mp", mp, 1 << bit), bit, 2 if bit else 1)
    return own


def input_grads(first_rows, other_rows, w_in, carried, start, width):
    rows, rest = first_rows.shape[1], other_rows.shape[1]
    features = w_in.shape[0]
    first, steps = start // BLOCK, width // BLOCK

    def kernel(*refs):
        own_ref, rest_ref, wi_ref = refs[:3]
        out_ref = refs[-1]
        step = pl.program_id(0)
        grad = jnp.concatenate([own_ref[0], rest_ref[0]], axis=0)
        value = contract(grad, wi_ref[...], 1, 1)

        @pl.when(step == 0)
        def _():
            out_ref[...] = value if carried is None else refs[3][...] + value

        @pl.when(step > 0)
        def _():
            out_ref[...] += value

    return pl.pallas_call(
        kernel,
        grid=(steps,),
        out_shape=jax.ShapeDtypeStruct((rows + rest, features), F32),
        in_specs=[
            pl.BlockSpec((1, rows, BLOCK), lambda i: (1, 0, first + i)),
            pl.BlockSpec((1, rest, BLOCK), lambda i: (1, 0, i)),
            pl.BlockSpec((features, BLOCK), lambda i: (0, first + i)),
        ]
        + ([] if carried is None else [whole(rows + rest, features)]),
        out_specs=whole(rows + rest, features),
        compiler_params=params(),
        cost_estimate=cost(
            2 * (rows + rest) * features * width, 2 * features * width
        ),
        name="input_grads",
    )(first_rows, other_rows, w_in, *([] if carried is None else [carried]))


def weight_grads(xt, gs, first_rows, others, factor):
    features, total = xt.shape
    hidden = first_rows.shape[2]
    rows, rest = first_rows.shape[1], others[0].shape[1]
    groups = len(others)
    steps = hidden // groups // BLOCK

    def kernel(xt_ref, gs_ref, act_ref, grad_ref, *refs):
        in_ref, out_ref = refs[-2:]
        step = pl.program_id(0)

        def work(rest_act_ref, rest_grad_ref):
            act = jnp.concatenate([act_ref[0], rest_act_ref[0]], axis=0)
            grad = jnp.concatenate([grad_ref[0], rest_grad_ref[0]], axis=0)
            turned = act.astype(F32).T.astype(BF16)
            in_ref[...] = (contract(xt_ref[...], grad, 1, 0) * factor).astype(BF16)
            out_ref[...] = (contract(turned, gs_ref[...], 1, 0) * factor).astype(BF16)

        for group in range(groups):
            here = (step >= group * steps) & (step < (group + 1) * steps)
            pl.when(here)(functools.partial(work, *refs[2 * group : 2 * group + 2]))

    def block(group, which):
        def place(i):
            return which, 0, jnp.clip(i - group * steps, 0, steps - 1)

        return pl.BlockSpec((1, rest, BLOCK), place)

    specs, operands = [], []
    for group, other in enumerate(others):
        specs += [block(group, 0), block(group, 1)]
        operands += [other, other]
    return pl.pallas_call(
        kernel,
        grid=(groups * steps,),
        out_shape=(
            jax.ShapeDtypeStruct((features, hidden), BF16),
            jax.ShapeDtypeStruct((hidden, features), BF16),
        ),
        in_specs=[
            whole(features, total),
            whole(total, features),
            pl.BlockSpec((1, rows, BLOCK), lambda i: (0, 0, i)),
            pl.BlockSpec((1, rows, BLOCK), lambda i: (1, 0, i)),
        ]
        + specs,
        out_specs=(
            pl.BlockSpec((features, BLOCK), lambda i: (0, i)),
            pl.BlockSpec((BLOCK, features), lambda i: (i, 0)),
        ),
        compiler_params=params(),
        cost_estimate=cost(4 * total * features * hidden, 4 * features * hidden),
        name="weight_grads",
    )(xt, gs, first_rows, first_rows, *operands)


def local(inputs, out_grads, w_in, w_out, dp, mp):
    hidden = w_in.shape[1]
    width = hidden // GROUPS
    rows = inputs.shape[0]
    total = rows * dp
    factor = 1.0 / math.sqrt(total)
    rank = lax.axis_index("mp").astype(jnp.int32).reshape(1)

    own = jnp.stack([inputs, out_grads])
    others = [exchange(own, "dp", dp, j) for j in range(1, dp)]

    keep, send = forward(rank, [own], w_in, w_out, 0, hidden)
    first_rows = reduce_and_activate(rank, keep, send, mp)
    other_rows = []
    for group in range(GROUPS):
        keep, send = forward(rank, others, w_in, w_out, group * width, width)
        other_rows.append(reduce_and_activate(rank, keep, send, mp))

    partial = None
    for group, other in enumerate(other_rows):
        partial = input_grads(first_rows, other, w_in, partial, group * width, width)
    in_total = partial[:rows]
    for j in range(1, dp):
        part = partial[j * rows : (j + 1) * rows].astype(BF16)
        in_total = in_total + exchange(part, "dp", dp, j).astype(F32)

    tokens = jnp.concatenate([own, *others], axis=1)
    unit = jnp.eye(total, dtype=BF16)
    xt = contract(tokens[0], unit, 0, 1).astype(BF16)
    grads = weight_grads(xt, tokens[1], first_rows, other_rows, factor)
    return (in_total, *grads)


def solution(mesh):
    sizes = dict(mesh.shape)
    return jax.shard_map(
        functools.partial(local, dp=sizes["dp"], mp=sizes["mp"]),
        mesh=mesh,
        in_specs=(P("dp", "mp"), P("dp", "mp"), P("mp", "dp"), P("dp", "mp")),
        out_specs=(P("dp", "mp"), P("mp", "dp"), P("dp", "mp")),
        check_vma=False,
    )
```

```python
import functools
import math

import jax
import jax.numpy as jnp
from jax import lax
from jax.experimental import pallas as pl
from jax.experimental.pallas import tpu as pltpu
from jax.sharding import PartitionSpec as P

BF16 = jnp.bfloat16
F32 = jnp.float32
GROUPS = 3
BLOCK = 512
SHARE = 1
VMEM_BYTES = 48 * 1024 * 1024
SMALL_BYTES = 16 * 1024 * 1024
SCALAR = pl.BlockSpec(memory_space=pltpu.SMEM)
ANY = pl.BlockSpec(memory_space=pl.ANY)


def gelu_parts(preact):
    cumul = 0.5 * (1.0 + jax.scipy.special.erf(preact * (1.0 / math.sqrt(2.0))))
    density = jnp.exp(-0.5 * preact * preact) * (1.0 / math.sqrt(2.0 * math.pi))
    return (preact * cumul, cumul + preact * density)


def contract(left, right, left_dim, right_dim):
    return lax.dot_general(
        left,
        right,
        (((left_dim,), (right_dim,)), ((), ())),
        preferred_element_type=F32,
    )


def exchange(array, axis, size, step):
    return lax.ppermute(array, axis, [(i, i ^ step) for i in range(size)])


def whole(*shape):
    return pl.BlockSpec(shape, lambda step: (0,) * len(shape))


def params(size=VMEM_BYTES):
    return pltpu.CompilerParams(vmem_limit_bytes=size)


def cost(flops, size):
    return pl.CostEstimate(
        flops=flops // SHARE, bytes_accessed=size // SHARE, transcendentals=0
    )


def by_bit(rank_ref, bit, choose):
    side = (rank_ref[0] >> bit) & 1
    for value in range(2):
        pl.when(side == value)(functools.partial(choose, value))


def forward(rank, tokens, w_in, w_out, start, width, after=()):
    parts = len(tokens)
    rows, features = tokens[0].shape[1:]
    total = parts * rows
    half = total // 2
    first, steps = start // BLOCK, width // BLOCK

    def kernel(rank_ref, *refs):
        token_refs = refs[:parts]
        wi_ref, wo_ref = refs[parts : parts + 2]
        keep_ref, send_ref = refs[-2:]

        def rows_of(which):
            return jnp.concatenate([ref[which] for ref in token_refs], axis=0)

        sums = (
            contract(rows_of(0), wi_ref[...], 1, 0),
            contract(wo_ref[...], rows_of(1), 1, 1).T,
        )

        def choose(core):
            for which, value in enumerate(sums):
                halves = value[:half], value[half:]
                keep_ref[which] = halves[core]
                send_ref[which] = halves[1 - core].astype(BF16)

        by_bit(rank_ref, 0, choose)

    block = pl.BlockSpec((2, half, BLOCK), lambda i: (0, 0, i))
    return pl.pallas_call(
        kernel,
        grid=(steps,),
        out_shape=(
            jax.ShapeDtypeStruct((2, half, width), F32),
            jax.ShapeDtypeStruct((2, half, width), BF16),
        ),
        in_specs=[SCALAR]
        + [whole(2, rows, features)] * parts
        + [
            pl.BlockSpec((features, BLOCK), lambda i: (0, first + i)),
            pl.BlockSpec((BLOCK, features), lambda i: (first + i, 0)),
        ]
        + [ANY] * len(after),
        out_specs=(block, block),
        compiler_params=params(),
        cost_estimate=cost(4 * total * features * width, 4 * features * width),
        name="forward",
    )(rank, *tokens, w_in, w_out, *after)


def halve(rank, keep, received, bit, after=()):
    _, rows, width = keep.shape
    half = width // 2

    def kernel(rank_ref, keep_ref, received_ref, *rest):
        next_ref, send_ref = rest[-2:]

        def choose(side):
            mine = slice(side * half, (side + 1) * half)
            other = slice((1 - side) * half, (2 - side) * half)
            next_ref[...] = keep_ref[:, :, mine] + received_ref[:, :, mine].astype(F32)
            send_ref[...] = (
                keep_ref[:, :, other] + received_ref[:, :, other].astype(F32)
            ).astype(BF16)

        by_bit(rank_ref, bit, choose)

    return pl.pallas_call(
        kernel,
        grid=(1,),
        out_shape=(
            jax.ShapeDtypeStruct((2, rows, half), F32),
            jax.ShapeDtypeStruct((2, rows, half), BF16),
        ),
        in_specs=[SCALAR] + [whole(2, rows, width)] * 2 + [ANY] * len(after),
        out_specs=(whole(2, rows, half),) * 2,
        compiler_params=params(SMALL_BYTES),
        cost_estimate=cost(2 * rows * width, 12 * rows * width),
        name="halve",
    )(rank, keep, received, *after)


def activate(keep, received, after=()):
    def kernel(keep_ref, received_ref, *rest):
        out_ref = rest[-1]
        value, slope = gelu_parts(keep_ref[0] + received_ref[0].astype(F32))
        grad = keep_ref[1] + received_ref[1].astype(F32)
        out_ref[0] = value.astype(BF16)
        out_ref[1] = (grad * slope).astype(BF16)

    return pl.pallas_call(
        kernel,
        grid=(1,),
        out_shape=jax.ShapeDtypeStruct(keep.shape, BF16),
        in_specs=[whole(*keep.shape)] * 2 + [ANY] * len(after),
        out_specs=whole(*keep.shape),
        compiler_params=params(SMALL_BYTES),
        cost_estimate=cost(20 * keep.size, 8 * keep.size),
        name="activate",
    )(keep, received, *after)


def relay(array, after):
    def kernel(in_ref, *rest):
        rest[-1][...] = in_ref[...]

    return pl.pallas_call(
        kernel,
        grid=(1,),
        out_shape=jax.ShapeDtypeStruct(array.shape, array.dtype),
        in_specs=[whole(*array.shape)] + [ANY] * len(after),
        out_specs=whole(*array.shape),
        compiler_params=params(SMALL_BYTES),
        cost_estimate=cost(0, 4 * array.size),
        name="relay",
    )(array, *after)


def join(rank, own, received, bit, axis, after=()):
    shape = list(own.shape)
    half = shape[axis]
    shape[axis] = 2 * half

    def kernel(rank_ref, own_ref, received_ref, *rest):
        out_ref = rest[-1]

        def choose(side):
            for place, source in ((side, own_ref), (1 - side, received_ref)):
                at = [slice(None)] * 3
                at[axis] = slice(place * half, (place + 1) * half)
                out_ref[tuple(at)] = source[...]

        by_bit(rank_ref, bit, choose)

    return pl.pallas_call(
        kernel,
        grid=(1,),
        out_shape=jax.ShapeDtypeStruct(shape, BF16),
        in_specs=[SCALAR] + [whole(*own.shape)] * 2 + [ANY] * len(after),
        out_specs=whole(*shape),
        compiler_params=params(SMALL_BYTES),
        cost_estimate=cost(0, 8 * own.size),
        name="join",
    )(rank, own, received, *after)


class Chunk:
    def __init__(self, rank, mp):
        self.rank, self.mp, self.bits = rank, mp, mp.bit_length() - 1
        self.keep, self.send, self.level = None, None, 0

    def advance(self, after):
        level, self.level = self.level, self.level + 1
        bit = level if level < self.bits else 2 * self.bits - 1 - level
        received = exchange(self.send, "mp", self.mp, 1 << bit)
        if level < self.bits - 1:
            self.keep, self.send = halve(self.rank, self.keep, received, bit + 1, after)
        elif level == self.bits - 1:
            self.send = activate(self.keep, received, after)
        else:
            axis = 2 if bit else 1
            self.send = join(self.rank, self.send, received, bit, axis, after)


def input_grads(
    first_rows, offset, other_rows, w_in, carried, start, width, last
):
    rows, rest = first_rows.shape[1], other_rows.shape[1]
    features = w_in.shape[0]
    first, steps = start // BLOCK, width // BLOCK
    shift = offset // BLOCK
    shape = (features, rows + rest)

    def kernel(*refs):
        own_ref, rest_ref, wi_ref = refs[:3]
        out_ref, sum_ref = refs[-2:]
        step = pl.program_id(0)
        grad = jnp.concatenate([own_ref[0], rest_ref[0]], axis=0)
        value = contract(wi_ref[...], grad, 1, 1)

        @pl.when(step == 0)
        def _():
            sum_ref[...] = value if carried is None else refs[3][...] + value

        @pl.when(step > 0)
        def _():
            sum_ref[...] += value

        @pl.when(step == steps - 1)
        def _():
            out_ref[...] = sum_ref[...].T if last else sum_ref[...]

    out = shape[::-1] if last else shape
    return pl.pallas_call(
        kernel,
        grid=(steps,),
        out_shape=jax.ShapeDtypeStruct(out, F32),
        in_specs=[
            pl.BlockSpec((1, rows, BLOCK), lambda i: (1, 0, shift + i)),
            pl.BlockSpec((1, rest, BLOCK), lambda i: (1, 0, i)),
            pl.BlockSpec((features, BLOCK), lambda i: (0, first + i)),
        ]
        + ([] if carried is None else [whole(*shape)]),
        out_specs=whole(*out),
        scratch_shapes=[pltpu.VMEM(shape, F32)],
        compiler_params=params(),
        cost_estimate=cost(
            2 * (rows + rest) * features * width, 2 * features * width
        ),
        name="input_grads",
    )(first_rows, other_rows, w_in, *([] if carried is None else [carried]))


def weight_grads(xt, gs, firsts, others, factor):
    features, total = xt.shape
    hidden = sum(part.shape[2] for part in firsts)

    def spans(arrays):
        end, found = 0, []
        for array in arrays:
            start, end = end, end + array.shape[2] // BLOCK
            found.append((array, start, end))
        return found

    first_spans, other_spans = spans(firsts), spans(others)
    cuts = sorted({end for _, _, end in first_spans + other_spans} | {0})

    def kernel(xt_ref, gs_ref, *refs):
        in_ref, out_ref = refs[-2:]
        step = pl.program_id(0)
        pairs = list(zip(refs[0:-2:2], refs[1:-2:2]))

        def work(first, other):
            (act_a, grad_a), (act_b, grad_b) = first, other
            act = jnp.concatenate([act_a[0], act_b[0]], axis=0)
            grad = jnp.concatenate([grad_a[0], grad_b[0]], axis=0)
            turned = act.astype(F32).T.astype(BF16)
            in_ref[...] = (contract(xt_ref[...], grad, 1, 0) * factor).astype(BF16)
            out_ref[...] = (contract(turned, gs_ref[...], 1, 0) * factor).astype(BF16)

        def holder(found, at, base):
            for index, (_, start, end) in enumerate(found):
                if start <= at < end:
                    return pairs[base + index]

        for low, high in zip(cuts[:-1], cuts[1:]):
            first = holder(first_spans, low, 0)
            other = holder(other_spans, low, len(firsts))
            here = (step >= low) & (step < high)
            pl.when(here)(functools.partial(work, first, other))

    def block(rows, start, end, which):
        def place(i):
            return which, 0, jnp.clip(i - start, 0, end - start - 1)

        return pl.BlockSpec((1, rows, BLOCK), place)

    specs, operands = [], []
    for array, start, end in first_spans + other_spans:
        specs += [block(array.shape[1], start, end, which) for which in range(2)]
        operands += [array, array]
    return pl.pallas_call(
        kernel,
        grid=(hidden // BLOCK,),
        out_shape=(
            jax.ShapeDtypeStruct((features, hidden), BF16),
            jax.ShapeDtypeStruct((hidden, features), BF16),
        ),
        in_specs=[whole(features, total), whole(total, features)] + specs,
        out_specs=(
            pl.BlockSpec((features, BLOCK), lambda i: (0, i)),
            pl.BlockSpec((BLOCK, features), lambda i: (i, 0)),
        ),
        compiler_params=params(),
        cost_estimate=cost(4 * total * features * hidden, 4 * features * hidden),
        name="weight_grads",
    )(xt, gs, *operands)


def local(inputs, out_grads, w_in, w_out, dp, mp):
    hidden = w_in.shape[1]
    width = hidden // GROUPS
    rows = inputs.shape[0]
    total = rows * dp
    factor = 1.0 / math.sqrt(total)
    rank = lax.axis_index("mp").astype(jnp.int32).reshape(1)

    own = jnp.stack([inputs, out_grads])
    others = [exchange(own, "dp", dp, j) for j in range(1, dp)]

    plans = [([own], 0, width), ([own], width, hidden - width)]
    plans += [(others, group * width, width) for group in range(GROUPS)]
    chunks = [Chunk(rank, mp) for _ in plans]
    levels = 2 * chunks[0].bits
    partial, after = None, []

    for slot in range(len(chunks) + levels):
        if slot < len(chunks):
            tokens, start, size = plans[slot]
            chunk = chunks[slot]
            chunk.keep, chunk.send = forward(
                rank, tokens, w_in, w_out, start, size, after
            )
            after = [chunk.send]
        for chunk in chunks[max(0, slot - levels) : slot]:
            early = slot < len(chunks)
            chunk.advance(after if early or chunk is chunks[-1] else [])
            after = [chunk.send] if early else after
        if 1 <= slot < len(chunks):
            chunks[slot].send = relay(chunks[slot].send, after)
            after = [chunks[slot].send]
        group = slot - levels - 2
        if group >= 0:
            first, offset = (0, 0) if group == 0 else (1, (group - 1) * width)
            partial = input_grads(
                chunks[first].send,
                offset,
                chunks[2 + group].send,
                w_in,
                partial,
                group * width,
                width,
                group == GROUPS - 1,
            )
            after = [partial]
    firsts = [chunk.send for chunk in chunks[:2]]
    finals = [chunk.send for chunk in chunks[2:]]

    in_total = partial[:rows]
    for j in range(1, dp):
        part = partial[j * rows : (j + 1) * rows].astype(BF16)
        in_total = in_total + exchange(part, "dp", dp, j).astype(F32)

    tokens = jnp.concatenate([own, *others], axis=1)
    unit = jnp.eye(total, dtype=BF16)
    xt = contract(tokens[0], unit, 0, 1).astype(BF16)
    grads = weight_grads(xt, tokens[1], firsts, finals, factor)
    return (in_total, *grads)


def solution(mesh):
    sizes = dict(mesh.shape)
    return jax.shard_map(
        functools.partial(local, dp=sizes["dp"], mp=sizes["mp"]),
        mesh=mesh,
        in_specs=(P("dp", "mp"), P("dp", "mp"), P("mp", "dp"), P("dp", "mp")),
        out_specs=(P("dp", "mp"), P("mp", "dp"), P("dp", "mp")),
        check_vma=False,
    )
```

```python
import functools
import math

import jax
import jax.numpy as jnp
from jax import lax
from jax.experimental import pallas as pl
from jax.experimental.pallas import tpu as pltpu
from jax.sharding import PartitionSpec as P

BF16 = jnp.bfloat16
F32 = jnp.float32
LOAD_BYTES = 38 * 1024 * 1024
CHUNKS = 4
PIECE = 384
VMEM_BYTES = 40 * 1024 * 1024
SMALL_BYTES = 16 * 1024 * 1024
SCALAR = pl.BlockSpec(memory_space=pltpu.SMEM)
ANY = pl.BlockSpec(memory_space=pl.ANY)
HBM = pl.BlockSpec(memory_space=pltpu.HBM)
VMEM = pl.BlockSpec(memory_space=pltpu.VMEM)


def gelu_parts(preact):
    cumul = 0.5 * (1.0 + jax.scipy.special.erf(preact * (1.0 / math.sqrt(2.0))))
    density = jnp.exp(-0.5 * preact * preact) * (1.0 / math.sqrt(2.0 * math.pi))
    return (preact * cumul, cumul + preact * density)


def contract(left, right, left_dim, right_dim):
    return lax.dot_general(
        left,
        right,
        (((left_dim,), (right_dim,)), ((), ())),
        preferred_element_type=F32,
    )


def exchange(array, axis, size, step):
    return lax.ppermute(array, axis, [(i, i ^ step) for i in range(size)])


def partner_step(level):
    return (1, 2, 6)[level] if level < 3 else 1 << level


def whole(*shape):
    return pl.BlockSpec(shape, lambda step: (0,) * len(shape))


def params(size=VMEM_BYTES):
    return pltpu.CompilerParams(vmem_limit_bytes=size)


def cost(flops, size):
    return pl.CostEstimate(
        flops=flops, bytes_accessed=size, transcendentals=0
    )


def by_side(rank_ref, level, choose):
    rank = rank_ref[0]
    side = (rank >> level) & 1
    if level == 1:
        side ^= (rank >> 2) & 1
    for value in range(2):
        pl.when(side == value)(functools.partial(choose, value))


def load(*weights):
    count = len(weights)

    def kernel(*refs):
        sources, targets, done = refs[:count], refs[count : 2 * count], refs[-1]
        copies = [
            pltpu.make_async_copy(source, target, done.at[index])
            for index, (source, target) in enumerate(zip(sources, targets))
        ]
        for copy in copies:
            copy.start()
        for copy in copies:
            copy.wait()

    return pl.pallas_call(
        kernel,
        out_shape=tuple(jax.ShapeDtypeStruct(w.shape, w.dtype) for w in weights),
        in_specs=[HBM] * count,
        out_specs=(VMEM,) * count,
        scratch_shapes=[pltpu.SemaphoreType.DMA((count,))],
        compiler_params=params(LOAD_BYTES),
        cost_estimate=cost(0, 4 * sum(w.size for w in weights)),
        name="load",
    )(*weights)


def pieces(start, width):
    return [(at, at + PIECE) for at in range(start, start + width, PIECE)]


def forward(rank, tokens, w_in, w_out, start, width, after=()):
    parts = len(tokens)
    rows, features = tokens[0].shape[1:]
    total = parts * rows
    half = total // 2

    def kernel(rank_ref, *refs):
        token_refs = refs[:parts]
        wi_ref, wo_ref = refs[parts : parts + 2]
        keep_ref, send_ref = refs[-2:]

        def rows_of(which):
            return jnp.concatenate([ref[which] for ref in token_refs], axis=0)

        for low, high in pieces(start, width):
            at = slice(low - start, high - start)
            sums = (
                contract(rows_of(0), wi_ref[:, low:high], 1, 0),
                contract(rows_of(1), wo_ref[low:high, :], 1, 1),
            )

            def choose(core, at=at, sums=sums):
                for which, value in enumerate(sums):
                    halves = value[:half], value[half:]
                    keep_ref[which, :, at] = halves[core]
                    send_ref[which, :, at] = halves[1 - core].astype(BF16)

            by_side(rank_ref, 0, choose)

    return pl.pallas_call(
        kernel,
        grid=(1,),
        out_shape=(
            jax.ShapeDtypeStruct((2, half, width), F32),
            jax.ShapeDtypeStruct((2, half, width), BF16),
        ),
        in_specs=[SCALAR]
        + [whole(2, rows, features)] * parts
        + [VMEM, VMEM]
        + [ANY] * len(after),
        out_specs=(whole(2, half, width),) * 2,
        compiler_params=params(SMALL_BYTES),
        cost_estimate=cost(4 * total * features * width, 4 * features * width),
        name="forward",
    )(rank, *tokens, w_in, w_out, *after)


def halve(rank, keep, received, level, after=()):
    _, rows, width = keep.shape
    half = rows // 2

    def kernel(rank_ref, keep_ref, received_ref, *rest):
        next_ref, send_ref = rest[-2:]

        def choose(side):
            mine = slice(side * half, (side + 1) * half)
            other = slice((1 - side) * half, (2 - side) * half)
            next_ref[...] = keep_ref[:, mine] + received_ref[:, mine].astype(F32)
            send_ref[...] = (
                keep_ref[:, other] + received_ref[:, other].astype(F32)
            ).astype(BF16)

        by_side(rank_ref, level, choose)

    return pl.pallas_call(
        kernel,
        grid=(1,),
        out_shape=(
            jax.ShapeDtypeStruct((2, half, width), F32),
            jax.ShapeDtypeStruct((2, half, width), BF16),
        ),
        in_specs=[SCALAR] + [whole(2, rows, width)] * 2 + [ANY] * len(after),
        out_specs=(whole(2, half, width),) * 2,
        compiler_params=params(SMALL_BYTES),
        cost_estimate=cost(2 * rows * width, 12 * rows * width),
        name="halve",
    )(rank, keep, received, *after)


def activate(keep, received, after=()):
    def kernel(keep_ref, received_ref, *rest):
        out_ref = rest[-1]
        value, slope = gelu_parts(keep_ref[0] + received_ref[0].astype(F32))
        grad = keep_ref[1] + received_ref[1].astype(F32)
        out_ref[0] = value.astype(BF16)
        out_ref[1] = (grad * slope).astype(BF16)

    return pl.pallas_call(
        kernel,
        grid=(1,),
        out_shape=jax.ShapeDtypeStruct(keep.shape, BF16),
        in_specs=[whole(*keep.shape)] * 2 + [ANY] * len(after),
        out_specs=whole(*keep.shape),
        compiler_params=params(SMALL_BYTES),
        cost_estimate=cost(20 * keep.size, 8 * keep.size),
        name="activate",
    )(keep, received, *after)


def relay(array, after):
    def kernel(in_ref, *rest):
        rest[-1][...] = in_ref[...]

    return pl.pallas_call(
        kernel,
        grid=(1,),
        out_shape=jax.ShapeDtypeStruct(array.shape, array.dtype),
        in_specs=[whole(*array.shape)] + [ANY] * len(after),
        out_specs=whole(*array.shape),
        compiler_params=params(SMALL_BYTES),
        cost_estimate=cost(0, 4 * array.size),
        name="relay",
    )(array, *after)


def join(rank, own, received, level, after=()):
    _, half, width = own.shape

    def kernel(rank_ref, own_ref, received_ref, *rest):
        out_ref = rest[-1]

        def choose(side):
            out_ref[:, side * half : (side + 1) * half] = own_ref[...]
            out_ref[:, (1 - side) * half : (2 - side) * half] = received_ref[...]

        by_side(rank_ref, level, choose)

    return pl.pallas_call(
        kernel,
        grid=(1,),
        out_shape=jax.ShapeDtypeStruct((2, 2 * half, width), BF16),
        in_specs=[SCALAR] + [whole(2, half, width)] * 2 + [ANY] * len(after),
        out_specs=whole(2, 2 * half, width),
        compiler_params=params(SMALL_BYTES),
        cost_estimate=cost(0, 8 * own.size),
        name="join",
    )(rank, own, received, *after)


class Chunk:
    def __init__(self, rank, mp, keep, send):
        self.rank, self.mp, self.levels = rank, mp, mp.bit_length() - 1
        self.keep, self.send, self.done = keep, send, 0

    def advance(self, after=()):
        index, self.done = self.done, self.done + 1
        level = min(index, 2 * self.levels - 1 - index)
        received = exchange(self.send, "mp", self.mp, partner_step(level))
        if index < self.levels - 1:
            self.keep, self.send = halve(
                self.rank, self.keep, received, level + 1, after
            )
        elif index == self.levels - 1:
            self.send = activate(self.keep, received, after)
        else:
            self.send = join(self.rank, self.send, received, level, after)
        return self.send

    def reach(self, done):
        while self.done < done:
            self.advance()


def input_grads(grads, w_in, carried, start):
    _, total, width = grads.shape
    features = w_in.shape[0]
    before = [] if carried is None else [carried]

    def kernel(grad_ref, wi_ref, *refs):
        value = refs[0][...] if before else 0.0
        for low, high in pieces(start, width):
            block = grad_ref[1, :, low - start : high - start]
            value = value + contract(block, wi_ref[:, low:high], 1, 1)
        refs[-1][...] = value

    return pl.pallas_call(
        kernel,
        grid=(1,),
        out_shape=jax.ShapeDtypeStruct((total, features), F32),
        in_specs=[whole(2, total, width), VMEM] + [whole(total, features)] * len(before),
        out_specs=whole(total, features),
        compiler_params=params(SMALL_BYTES),
        cost_estimate=cost(2 * total * features * width, 2 * features * width),
        name="input_grads",
    )(grads, w_in, *before)


def weight_grads(xt, gs, finals, factor):
    features, total = xt.shape
    width = finals[0].shape[2]
    hidden = width * len(finals)

    def kernel(xt_ref, gs_ref, *refs):
        in_ref, out_ref = refs[-2:]
        step = pl.program_id(0)

        def work(final_ref):
            for low, high in pieces(0, width):
                act, grad = final_ref[0, :, low:high], final_ref[1, :, low:high]
                turned = act.astype(F32).T.astype(BF16)
                in_ref[:, low:high] = (contract(xt_ref[...], grad, 1, 0) * factor).astype(BF16)
                out_ref[low:high, :] = (contract(turned, gs_ref[...], 1, 0) * factor).astype(BF16)

        for index in range(len(finals)):
            pl.when(step == index)(functools.partial(work, refs[index]))

    return pl.pallas_call(
        kernel,
        grid=(len(finals),),
        out_shape=(
            jax.ShapeDtypeStruct((features, hidden), BF16),
            jax.ShapeDtypeStruct((hidden, features), BF16),
        ),
        in_specs=[whole(features, total), whole(total, features)]
        + [whole(2, total, width)] * len(finals),
        out_specs=(
            pl.BlockSpec((features, width), lambda i: (0, i)),
            pl.BlockSpec((width, features), lambda i: (i, 0)),
        ),
        compiler_params=params(),
        cost_estimate=cost(4 * total * features * hidden, 4 * features * hidden),
        name="weight_grads",
    )(xt, gs, *finals)


def local(inputs, out_grads, w_in, w_out, dp, mp):
    hidden = w_in.shape[1]
    rows = inputs.shape[0]
    total = rows * dp
    factor = 1.0 / math.sqrt(total)
    rank = lax.axis_index("mp").astype(jnp.int32).reshape(1)
    width = hidden // CHUNKS
    starts = [index * width for index in range(CHUNKS)]

    own = jnp.stack([inputs, out_grads])
    parts = [own] + [exchange(own, "dp", dp, j) for j in range(1, dp)]

    w_in, w_out = load(w_in, w_out)

    chunks, after = [], []
    for start in starts:
        keep, send = forward(rank, parts, w_in, w_out, start, width, after)
        after = [send]
        for chunk in chunks[::-1]:
            after = [chunk.advance(after)]
        if chunks:
            after = [relay(send, after)]
            send = after[0]
        chunks.append(Chunk(rank, mp, keep, send))

    steps = 2 * chunks[0].levels
    partials, partial = [], None
    for index, (start, chunk) in enumerate(zip(starts, chunks)):
        chunk.reach(steps - 2)
        chunk.advance(partials[index - 2 : index - 1] if index > 1 else [])
        chunk.advance(partials[index - 1 :])
        partial = input_grads(chunk.send, w_in, partial, start)
        partials.append(partial)
    finals = [chunk.send for chunk in chunks]

    in_total = partial[:rows]
    for j in range(1, dp):
        part = partial[j * rows : (j + 1) * rows].astype(BF16)
        in_total = in_total + exchange(part, "dp", dp, j).astype(F32)

    tokens = jnp.concatenate(parts, axis=1)
    unit = jnp.eye(total, dtype=BF16)
    xt = contract(tokens[0], unit, 0, 1).astype(BF16)
    return (in_total, *weight_grads(xt, tokens[1], finals, factor))


def solution(mesh):
    sizes = dict(mesh.shape)
    return jax.shard_map(
        functools.partial(local, dp=sizes["dp"], mp=sizes["mp"]),
        mesh=mesh,
        in_specs=(P("dp", "mp"), P("dp", "mp"), P("mp", "dp"), P("dp", "mp")),
        out_specs=(P("dp", "mp"), P("mp", "dp"), P("dp", "mp")),
        check_vma=False,
    )
```

```python
import functools
import math

import jax
import jax.numpy as jnp
from jax import lax
from jax.experimental import pallas as pl
from jax.experimental.pallas import tpu as pltpu
from jax.sharding import PartitionSpec as P

BF16 = jnp.bfloat16
F32 = jnp.float32
LOAD_BYTES = 24 * 1024 * 1024
CHUNKS = 3
PIECE = 384
VMEM_BYTES = 40 * 1024 * 1024
SMALL_BYTES = 16 * 1024 * 1024
SCALAR = pl.BlockSpec(memory_space=pltpu.SMEM)
ANY = pl.BlockSpec(memory_space=pl.ANY)
HBM = pl.BlockSpec(memory_space=pltpu.HBM)
VMEM = pl.BlockSpec(memory_space=pltpu.VMEM)


def gelu_parts(preact):
    cumul = 0.5 * (1.0 + jax.scipy.special.erf(preact * (1.0 / math.sqrt(2.0))))
    density = jnp.exp(-0.5 * preact * preact) * (1.0 / math.sqrt(2.0 * math.pi))
    return (preact * cumul, cumul + preact * density)


def contract(left, right, left_dim, right_dim):
    return lax.dot_general(
        left,
        right,
        (((left_dim,), (right_dim,)), ((), ())),
        preferred_element_type=F32,
    )


def exchange(array, axis, size, step):
    return lax.ppermute(array, axis, [(i, i ^ step) for i in range(size)])


def partner_step(level):
    return (1, 2, 6)[level] if level < 3 else 1 << level


def whole(*shape):
    return pl.BlockSpec(shape, lambda step: (0,) * len(shape))


def params(size=VMEM_BYTES):
    return pltpu.CompilerParams(vmem_limit_bytes=size)


def cost(flops, size):
    return pl.CostEstimate(
        flops=flops, bytes_accessed=size, transcendentals=0
    )


def by_side(rank_ref, level, choose):
    rank = rank_ref[0]
    side = (rank >> level) & 1
    if level == 1:
        side ^= (rank >> 2) & 1
    for value in range(2):
        pl.when(side == value)(functools.partial(choose, value))


def load(*weights):
    count = len(weights)

    def kernel(*refs):
        sources, targets, done = refs[:count], refs[count : 2 * count], refs[-1]
        copies = [
            pltpu.make_async_copy(source, target, done.at[index])
            for index, (source, target) in enumerate(zip(sources, targets))
        ]
        for copy in copies:
            copy.start()
        for copy in copies:
            copy.wait()

    return pl.pallas_call(
        kernel,
        out_shape=tuple(jax.ShapeDtypeStruct(w.shape, w.dtype) for w in weights),
        in_specs=[HBM] * count,
        out_specs=(VMEM,) * count,
        scratch_shapes=[pltpu.SemaphoreType.DMA((count,))],
        compiler_params=params(LOAD_BYTES),
        cost_estimate=cost(0, 4 * sum(w.size for w in weights)),
        name="load",
    )(*weights)


def pieces(start, width):
    return [(at, at + PIECE) for at in range(start, start + width, PIECE)]


def forward(rank, tokens, w_in, w_out, start, width, after=()):
    parts = len(tokens)
    rows, features = tokens[0].shape[1:]
    total = parts * rows
    half = total // 2

    def kernel(rank_ref, *refs):
        token_refs = refs[:parts]
        wi_ref, wo_ref = refs[parts : parts + 2]
        keep_ref, send_ref = refs[-2:]

        def rows_of(which):
            return jnp.concatenate([ref[which] for ref in token_refs], axis=0)

        for low, high in pieces(start, width):
            at = slice(low - start, high - start)
            sums = (
                contract(rows_of(0), wi_ref[:, low:high], 1, 0),
                contract(rows_of(1), wo_ref[low:high, :], 1, 1),
            )

            def choose(core, at=at, sums=sums):
                for which, value in enumerate(sums):
                    halves = value[:half], value[half:]
                    keep_ref[which, :, at] = halves[core]
                    send_ref[which, :, at] = halves[1 - core].astype(BF16)

            by_side(rank_ref, 0, choose)

    return pl.pallas_call(
        kernel,
        grid=(1,),
        out_shape=(
            jax.ShapeDtypeStruct((2, half, width), F32),
            jax.ShapeDtypeStruct((2, half, width), BF16),
        ),
        in_specs=[SCALAR]
        + [whole(2, rows, features)] * parts
        + [VMEM, VMEM]
        + [ANY] * len(after),
        out_specs=(whole(2, half, width),) * 2,
        compiler_params=params(SMALL_BYTES),
        cost_estimate=cost(4 * total * features * width, 4 * features * width),
        name="forward",
    )(rank, *tokens, w_in, w_out, *after)


def halve(rank, keep, received, level, after=()):
    _, rows, width = keep.shape
    half = rows // 2

    def kernel(rank_ref, keep_ref, received_ref, *rest):
        next_ref, send_ref = rest[-2:]

        def choose(side):
            mine = slice(side * half, (side + 1) * half)
            other = slice((1 - side) * half, (2 - side) * half)
            next_ref[...] = keep_ref[:, mine] + received_ref[:, mine].astype(F32)
            send_ref[...] = (
                keep_ref[:, other] + received_ref[:, other].astype(F32)
            ).astype(BF16)

        by_side(rank_ref, level, choose)

    return pl.pallas_call(
        kernel,
        grid=(1,),
        out_shape=(
            jax.ShapeDtypeStruct((2, half, width), F32),
            jax.ShapeDtypeStruct((2, half, width), BF16),
        ),
        in_specs=[SCALAR] + [whole(2, rows, width)] * 2 + [ANY] * len(after),
        out_specs=(whole(2, half, width),) * 2,
        compiler_params=params(SMALL_BYTES),
        cost_estimate=cost(2 * rows * width, 12 * rows * width),
        name="halve",
    )(rank, keep, received, *after)


def activate(keep, received, after=()):
    def kernel(keep_ref, received_ref, *rest):
        out_ref = rest[-1]
        value, slope = gelu_parts(keep_ref[0] + received_ref[0].astype(F32))
        grad = keep_ref[1] + received_ref[1].astype(F32)
        out_ref[0] = value.astype(BF16)
        out_ref[1] = (grad * slope).astype(BF16)

    return pl.pallas_call(
        kernel,
        grid=(1,),
        out_shape=jax.ShapeDtypeStruct(keep.shape, BF16),
        in_specs=[whole(*keep.shape)] * 2 + [ANY] * len(after),
        out_specs=whole(*keep.shape),
        compiler_params=params(SMALL_BYTES),
        cost_estimate=cost(20 * keep.size, 8 * keep.size),
        name="activate",
    )(keep, received, *after)


def relay(array, after):
    def kernel(in_ref, *rest):
        rest[-1][...] = in_ref[...]

    return pl.pallas_call(
        kernel,
        grid=(1,),
        out_shape=jax.ShapeDtypeStruct(array.shape, array.dtype),
        in_specs=[whole(*array.shape)] + [ANY] * len(after),
        out_specs=whole(*array.shape),
        compiler_params=params(SMALL_BYTES),
        cost_estimate=cost(0, 4 * array.size),
        name="relay",
    )(array, *after)


def join(rank, own, received, level, after=()):
    _, half, width = own.shape

    def kernel(rank_ref, own_ref, received_ref, *rest):
        out_ref = rest[-1]

        def choose(side):
            out_ref[:, side * half : (side + 1) * half] = own_ref[...]
            out_ref[:, (1 - side) * half : (2 - side) * half] = received_ref[...]

        by_side(rank_ref, level, choose)

    return pl.pallas_call(
        kernel,
        grid=(1,),
        out_shape=jax.ShapeDtypeStruct((2, 2 * half, width), BF16),
        in_specs=[SCALAR] + [whole(2, half, width)] * 2 + [ANY] * len(after),
        out_specs=whole(2, 2 * half, width),
        compiler_params=params(SMALL_BYTES),
        cost_estimate=cost(0, 8 * own.size),
        name="join",
    )(rank, own, received, *after)


class Chunk:
    def __init__(self, rank, mp, keep, send):
        self.rank, self.mp, self.levels = rank, mp, mp.bit_length() - 1
        self.keep, self.send, self.done = keep, send, 0

    def advance(self, after=()):
        index, self.done = self.done, self.done + 1
        level = min(index, 2 * self.levels - 1 - index)
        received = exchange(self.send, "mp", self.mp, partner_step(level))
        if index < self.levels - 1:
            self.keep, self.send = halve(
                self.rank, self.keep, received, level + 1, after
            )
        elif index == self.levels - 1:
            self.send = activate(self.keep, received, after)
        else:
            self.send = join(self.rank, self.send, received, level, after)
        return self.send

    def reach(self, done):
        while self.done < done:
            self.advance()


def input_grads(grads, w_in, carried, start):
    _, total, width = grads.shape
    features = w_in.shape[0]
    before = [] if carried is None else [carried]

    def kernel(grad_ref, wi_ref, *refs):
        value = refs[0][...] if before else 0.0
        for low, high in pieces(start, width):
            block = grad_ref[1, :, low - start : high - start]
            value = value + contract(block, wi_ref[:, low:high], 1, 1)
        refs[-1][...] = value

    return pl.pallas_call(
        kernel,
        grid=(1,),
        out_shape=jax.ShapeDtypeStruct((total, features), F32),
        in_specs=[whole(2, total, width), VMEM] + [whole(total, features)] * len(before),
        out_specs=whole(total, features),
        compiler_params=params(SMALL_BYTES),
        cost_estimate=cost(2 * total * features * width, 2 * features * width),
        name="input_grads",
    )(grads, w_in, *before)


def weight_grads(xt, gs, finals, factor):
    features, total = xt.shape
    width = finals[0].shape[2] // 2
    hidden = 2 * width * len(finals)

    def kernel(xt_ref, gs_ref, *refs):
        in_ref, out_ref = refs[-2:]
        step = pl.program_id(0)

        def work(final_ref):
            for low, high in pieces(0, width):
                act, grad = final_ref[0, :, low:high], final_ref[1, :, low:high]
                turned = act.astype(F32).T.astype(BF16)
                in_ref[:, low:high] = (contract(xt_ref[...], grad, 1, 0) * factor).astype(BF16)
                out_ref[low:high, :] = (contract(turned, gs_ref[...], 1, 0) * factor).astype(BF16)

        for index in range(len(finals)):
            pl.when((step >= 2 * index) & (step < 2 * index + 2))(functools.partial(work, refs[index]))

    def block(index):
        def place(i):
            return 0, 0, jnp.clip(i - 2 * index, 0, 1)

        return pl.BlockSpec((2, total, width), place)

    return pl.pallas_call(
        kernel,
        grid=(2 * len(finals),),
        out_shape=(
            jax.ShapeDtypeStruct((features, hidden), BF16),
            jax.ShapeDtypeStruct((hidden, features), BF16),
        ),
        in_specs=[whole(features, total), whole(total, features)]
        + [block(index) for index in range(len(finals))],
        out_specs=(
            pl.BlockSpec((features, width), lambda i: (0, i)),
            pl.BlockSpec((width, features), lambda i: (i, 0)),
        ),
        compiler_params=params(),
        cost_estimate=cost(4 * total * features * hidden, 4 * features * hidden),
        name="weight_grads",
    )(xt, gs, *finals)


def local(inputs, out_grads, w_in, w_out, dp, mp):
    hidden = w_in.shape[1]
    rows = inputs.shape[0]
    total = rows * dp
    factor = 1.0 / math.sqrt(total)
    rank = lax.axis_index("mp").astype(jnp.int32).reshape(1)
    width = hidden // CHUNKS
    starts = [index * width for index in range(CHUNKS)]

    own = jnp.stack([inputs, out_grads])
    parts = [own] + [exchange(own, "dp", dp, j) for j in range(1, dp)]

    w_in, w_out = load(w_in, w_out)

    chunks, after = [], []
    for start in starts:
        keep, send = forward(rank, parts, w_in, w_out, start, width, after)
        after = [send]
        for chunk in chunks[::-1]:
            after = [chunk.advance(after)]
        if chunks:
            after = [relay(send, after)]
            send = after[0]
        chunks.append(Chunk(rank, mp, keep, send))

    steps = 2 * chunks[0].levels
    partials, partial = [], None
    for index, (start, chunk) in enumerate(zip(starts, chunks)):
        chunk.reach(steps - 2)
        chunk.advance(partials[index - 2 : index - 1] if index > 1 else [])
        chunk.advance(partials[index - 1 :])
        partial = input_grads(chunk.send, w_in, partial, start)
        partials.append(partial)
    finals = [chunk.send for chunk in chunks]

    in_total = partial[:rows]
    for j in range(1, dp):
        part = partial[j * rows : (j + 1) * rows].astype(BF16)
        in_total = in_total + exchange(part, "dp", dp, j).astype(F32)

    tokens = jnp.concatenate(parts, axis=1)
    unit = jnp.eye(total, dtype=BF16)
    xt = contract(tokens[0], unit, 0, 1).astype(BF16)
    return (in_total, *weight_grads(xt, tokens[1], finals, factor))


def solution(mesh):
    sizes = dict(mesh.shape)
    return jax.shard_map(
        functools.partial(local, dp=sizes["dp"], mp=sizes["mp"]),
        mesh=mesh,
        in_specs=(P("dp", "mp"), P("dp", "mp"), P("mp", "dp"), P("dp", "mp")),
        out_specs=(P("dp", "mp"), P("mp", "dp"), P("dp", "mp")),
        check_vma=False,
    )
```

```python
import functools
import math

import jax
import jax.numpy as jnp
from jax import lax
from jax.experimental import pallas as pl
from jax.experimental.pallas import tpu as pltpu
from jax.sharding import PartitionSpec as P

BF16 = jnp.bfloat16
F32 = jnp.float32
LOAD_BYTES = 24 * 1024 * 1024
CHUNKS = 3
PIECE = 384
VMEM_BYTES = 40 * 1024 * 1024
SMALL_BYTES = 16 * 1024 * 1024
SCALAR = pl.BlockSpec(memory_space=pltpu.SMEM)
ANY = pl.BlockSpec(memory_space=pl.ANY)
HBM = pl.BlockSpec(memory_space=pltpu.HBM)
VMEM = pl.BlockSpec(memory_space=pltpu.VMEM)


def gelu_parts(preact):
    cumul = 0.5 * (1.0 + jax.scipy.special.erf(preact * (1.0 / math.sqrt(2.0))))
    density = jnp.exp(-0.5 * preact * preact) * (1.0 / math.sqrt(2.0 * math.pi))
    return (preact * cumul, cumul + preact * density)


def contract(left, right, left_dim, right_dim):
    return lax.dot_general(
        left,
        right,
        (((left_dim,), (right_dim,)), ((), ())),
        preferred_element_type=F32,
    )


def exchange(array, axis, size, step):
    return lax.ppermute(array, axis, [(i, i ^ step) for i in range(size)])


def partner_step(level):
    return (1, 2, 6)[level] if level < 3 else 1 << level


def whole(*shape):
    return pl.BlockSpec(shape, lambda step: (0,) * len(shape))


def params(size=VMEM_BYTES):
    return pltpu.CompilerParams(vmem_limit_bytes=size)


def cost(flops, size):
    return pl.CostEstimate(
        flops=flops, bytes_accessed=size, transcendentals=0
    )


def by_side(rank_ref, level, choose):
    rank = rank_ref[0]
    side = (rank >> level) & 1
    if level == 1:
        side ^= (rank >> 2) & 1
    for value in range(2):
        pl.when(side == value)(functools.partial(choose, value))


def load(*weights):
    count = len(weights)

    def kernel(*refs):
        sources, targets, done = refs[:count], refs[count : 2 * count], refs[-1]
        copies = [
            pltpu.make_async_copy(source, target, done.at[index])
            for index, (source, target) in enumerate(zip(sources, targets))
        ]
        for copy in copies:
            copy.start()
        for copy in copies:
            copy.wait()

    return pl.pallas_call(
        kernel,
        out_shape=tuple(jax.ShapeDtypeStruct(w.shape, w.dtype) for w in weights),
        in_specs=[HBM] * count,
        out_specs=(VMEM,) * count,
        scratch_shapes=[pltpu.SemaphoreType.DMA((count,))],
        compiler_params=params(LOAD_BYTES),
        cost_estimate=cost(0, 4 * sum(w.size for w in weights)),
        name="load",
    )(*weights)


def pieces(start, width):
    return [(at, at + PIECE) for at in range(start, start + width, PIECE)]


def forward(rank, tokens, w_in, w_out, start, width, after=()):
    parts = len(tokens)
    rows, features = tokens[0].shape[1:]
    total = parts * rows
    half = total // 2

    def kernel(rank_ref, *refs):
        token_refs = refs[:parts]
        wi_ref, wo_ref = refs[parts : parts + 2]
        keep_ref, send_ref = refs[-2:]

        def rows_of(which):
            return jnp.concatenate([ref[which] for ref in token_refs], axis=0)

        for low, high in pieces(start, width):
            at = slice(low - start, high - start)
            sums = (
                contract(rows_of(0), wi_ref[:, low:high], 1, 0),
                contract(rows_of(1), wo_ref[low:high, :], 1, 1),
            )

            def choose(core, at=at, sums=sums):
                for which, value in enumerate(sums):
                    halves = value[:half], value[half:]
                    keep_ref[which, :, at] = halves[core]
                    send_ref[which, :, at] = halves[1 - core].astype(BF16)

            by_side(rank_ref, 0, choose)

    return pl.pallas_call(
        kernel,
        grid=(1,),
        out_shape=(
            jax.ShapeDtypeStruct((2, half, width), F32),
            jax.ShapeDtypeStruct((2, half, width), BF16),
        ),
        in_specs=[SCALAR]
        + [whole(2, rows, features)] * parts
        + [VMEM, VMEM]
        + [ANY] * len(after),
        out_specs=(whole(2, half, width),) * 2,
        compiler_params=params(SMALL_BYTES),
        cost_estimate=cost(4 * total * features * width, 4 * features * width),
        name="forward",
    )(rank, *tokens, w_in, w_out, *after)


def halve(rank, keep, received, level, after=()):
    _, rows, width = keep.shape
    half = rows // 2

    def kernel(rank_ref, keep_ref, received_ref, *rest):
        next_ref, send_ref = rest[-2:]

        def choose(side):
            mine = slice(side * half, (side + 1) * half)
            other = slice((1 - side) * half, (2 - side) * half)
            next_ref[...] = keep_ref[:, mine] + received_ref[:, mine].astype(F32)
            send_ref[...] = (
                keep_ref[:, other] + received_ref[:, other].astype(F32)
            ).astype(BF16)

        by_side(rank_ref, level, choose)

    return pl.pallas_call(
        kernel,
        grid=(1,),
        out_shape=(
            jax.ShapeDtypeStruct((2, half, width), F32),
            jax.ShapeDtypeStruct((2, half, width), BF16),
        ),
        in_specs=[SCALAR] + [whole(2, rows, width)] * 2 + [ANY] * len(after),
        out_specs=(whole(2, half, width),) * 2,
        compiler_params=params(SMALL_BYTES),
        cost_estimate=cost(2 * rows * width, 12 * rows * width),
        name="halve",
    )(rank, keep, received, *after)


def activate(keep, received, after=()):
    def kernel(keep_ref, received_ref, *rest):
        out_ref = rest[-1]
        value, slope = gelu_parts(keep_ref[0] + received_ref[0].astype(F32))
        grad = keep_ref[1] + received_ref[1].astype(F32)
        out_ref[0] = value.astype(BF16)
        out_ref[1] = (grad * slope).astype(BF16)

    return pl.pallas_call(
        kernel,
        grid=(1,),
        out_shape=jax.ShapeDtypeStruct(keep.shape, BF16),
        in_specs=[whole(*keep.shape)] * 2 + [ANY] * len(after),
        out_specs=whole(*keep.shape),
        compiler_params=params(SMALL_BYTES),
        cost_estimate=cost(20 * keep.size, 8 * keep.size),
        name="activate",
    )(keep, received, *after)


def relay(array, after):
    def kernel(in_ref, *rest):
        rest[-1][...] = in_ref[...]

    return pl.pallas_call(
        kernel,
        grid=(1,),
        out_shape=jax.ShapeDtypeStruct(array.shape, array.dtype),
        in_specs=[whole(*array.shape)] + [ANY] * len(after),
        out_specs=whole(*array.shape),
        compiler_params=params(SMALL_BYTES),
        cost_estimate=cost(0, 4 * array.size),
        name="relay",
    )(array, *after)


def join(rank, own, received, level, after=()):
    _, half, width = own.shape

    def kernel(rank_ref, own_ref, received_ref, *rest):
        out_ref = rest[-1]

        def choose(side):
            out_ref[:, side * half : (side + 1) * half] = own_ref[...]
            out_ref[:, (1 - side) * half : (2 - side) * half] = received_ref[...]

        by_side(rank_ref, level, choose)

    return pl.pallas_call(
        kernel,
        grid=(1,),
        out_shape=jax.ShapeDtypeStruct((2, 2 * half, width), BF16),
        in_specs=[SCALAR] + [whole(2, half, width)] * 2 + [ANY] * len(after),
        out_specs=whole(2, 2 * half, width),
        compiler_params=params(SMALL_BYTES),
        cost_estimate=cost(0, 8 * own.size),
        name="join",
    )(rank, own, received, *after)


class Chunk:
    def __init__(self, rank, mp, keep, send):
        self.rank, self.mp, self.levels = rank, mp, mp.bit_length() - 1
        self.keep, self.send, self.done = keep, send, 0

    def advance(self, after=()):
        index, self.done = self.done, self.done + 1
        level = min(index, 2 * self.levels - 1 - index)
        received = exchange(self.send, "mp", self.mp, partner_step(level))
        if index < self.levels - 1:
            self.keep, self.send = halve(
                self.rank, self.keep, received, level + 1, after
            )
        elif index == self.levels - 1:
            self.send = activate(self.keep, received, after)
        else:
            self.send = join(self.rank, self.send, received, level, after)
        return self.send

    def reach(self, done):
        while self.done < done:
            self.advance()


def input_grads(grads, w_in, carried, start):
    _, total, width = grads.shape
    features = w_in.shape[0]
    before = [] if carried is None else [carried]

    def kernel(grad_ref, wi_ref, *refs):
        value = refs[0][...] if before else 0.0
        for low, high in pieces(start, width):
            block = grad_ref[1, :, low - start : high - start]
            value = value + contract(block, wi_ref[:, low:high], 1, 1)
        refs[-1][...] = value

    return pl.pallas_call(
        kernel,
        grid=(1,),
        out_shape=jax.ShapeDtypeStruct((total, features), F32),
        in_specs=[whole(2, total, width), VMEM] + [whole(total, features)] * len(before),
        out_specs=whole(total, features),
        compiler_params=params(SMALL_BYTES),
        cost_estimate=cost(2 * total * features * width, 2 * features * width),
        name="input_grads",
    )(grads, w_in, *before)


def weight_grads(xt, gs, finals, factor):
    features, total = xt.shape
    width = finals[0].shape[2] // 2
    hidden = 2 * width * len(finals)

    def kernel(xt_ref, gs_ref, *refs):
        in_ref, out_ref = refs[-2:]
        step = pl.program_id(0)

        def work(final_ref):
            for low, high in pieces(0, width):
                act, grad = final_ref[0, :, low:high], final_ref[1, :, low:high]
                turned = act.astype(F32).T.astype(BF16)
                in_ref[:, low:high] = (contract(xt_ref[...], grad, 1, 0) * factor).astype(BF16)
                out_ref[low:high, :] = (contract(turned, gs_ref[...], 1, 0) * factor).astype(BF16)

        for index in range(len(finals)):
            pl.when((step >= 2 * index) & (step < 2 * index + 2))(functools.partial(work, refs[index]))

    def block(index):
        def place(i):
            return 0, 0, jnp.clip(i - 2 * index, 0, 1)

        return pl.BlockSpec((2, total, width), place)

    return pl.pallas_call(
        kernel,
        grid=(2 * len(finals),),
        out_shape=(
            jax.ShapeDtypeStruct((features, hidden), BF16),
            jax.ShapeDtypeStruct((hidden, features), BF16),
        ),
        in_specs=[whole(features, total), whole(total, features)]
        + [block(index) for index in range(len(finals))],
        out_specs=(
            pl.BlockSpec((features, width), lambda i: (0, i)),
            pl.BlockSpec((width, features), lambda i: (i, 0)),
        ),
        compiler_params=params(),
        cost_estimate=cost(4 * total * features * hidden, 4 * features * hidden),
        name="weight_grads",
    )(xt, gs, *finals)


def local(inputs, out_grads, w_in, w_out, dp, mp):
    hidden = w_in.shape[1]
    rows = inputs.shape[0]
    total = rows * dp
    factor = 1.0 / math.sqrt(total)
    rank = lax.axis_index("mp").astype(jnp.int32).reshape(1)
    width = hidden // CHUNKS
    starts = [index * width for index in range(CHUNKS)]

    own = jnp.stack([inputs, out_grads])
    parts = [own] + [exchange(own, "dp", dp, j) for j in range(1, dp)]

    w_in, w_out = load(w_in, w_out)

    chunks, after = [], []
    for start in starts:
        keep, send = forward(rank, parts, w_in, w_out, start, width, after)
        after = [send]
        for chunk in chunks[::-1]:
            after = [chunk.advance(after)]
        if chunks:
            after = [relay(send, after)]
            send = after[0]
        chunks.append(Chunk(rank, mp, keep, send))

    steps = 2 * chunks[0].levels
    partial = None
    while chunks[-1].done < steps:
        for chunk in chunks[::-1]:
            if chunk.done < steps:
                after = [chunk.advance(after)]
                if chunk.done == steps:
                    start = starts[chunks.index(chunk)]
                    partial = input_grads(chunk.send, w_in, partial, start)
                    after = [partial]
    finals = [chunk.send for chunk in chunks]

    in_total = partial[:rows]
    for j in range(1, dp):
        part = partial[j * rows : (j + 1) * rows].astype(BF16)
        in_total = in_total + exchange(part, "dp", dp, j).astype(F32)

    tokens = jnp.concatenate(parts, axis=1)
    unit = jnp.eye(total, dtype=BF16)
    xt = contract(tokens[0], unit, 0, 1).astype(BF16)
    return (in_total, *weight_grads(xt, tokens[1], finals, factor))


def solution(mesh):
    sizes = dict(mesh.shape)
    return jax.shard_map(
        functools.partial(local, dp=sizes["dp"], mp=sizes["mp"]),
        mesh=mesh,
        in_specs=(P("dp", "mp"), P("dp", "mp"), P("mp", "dp"), P("dp", "mp")),
        out_specs=(P("dp", "mp"), P("mp", "dp"), P("dp", "mp")),
        check_vma=False,
    )
```

```python
import functools
import math

import jax
import jax.numpy as jnp
from jax import lax
from jax.experimental import pallas as pl
from jax.experimental.pallas import tpu as pltpu
from jax.sharding import PartitionSpec as P

BF16 = jnp.bfloat16
F32 = jnp.float32
LOAD_BYTES = 24 * 1024 * 1024
CHUNKS = 3
PIECE = 384
VMEM_BYTES = 40 * 1024 * 1024
SMALL_BYTES = 16 * 1024 * 1024
SCALAR = pl.BlockSpec(memory_space=pltpu.SMEM)
ANY = pl.BlockSpec(memory_space=pl.ANY)
HBM = pl.BlockSpec(memory_space=pltpu.HBM)
VMEM = pl.BlockSpec(memory_space=pltpu.VMEM)


def gelu_parts(preact):
    cumul = 0.5 * (1.0 + jax.scipy.special.erf(preact * (1.0 / math.sqrt(2.0))))
    density = jnp.exp(-0.5 * preact * preact) * (1.0 / math.sqrt(2.0 * math.pi))
    return (preact * cumul, cumul + preact * density)


def contract(left, right, left_dim, right_dim):
    return lax.dot_general(
        left,
        right,
        (((left_dim,), (right_dim,)), ((), ())),
        preferred_element_type=F32,
    )


def exchange(array, axis, size, step):
    return lax.ppermute(array, axis, [(i, i ^ step) for i in range(size)])


def partner_step(level):
    return (1, 2, 6)[level] if level < 3 else 1 << level


def whole(*shape):
    return pl.BlockSpec(shape, lambda step: (0,) * len(shape))


def params(size=VMEM_BYTES):
    return pltpu.CompilerParams(vmem_limit_bytes=size)


def cost(flops, size):
    return pl.CostEstimate(
        flops=flops, bytes_accessed=size, transcendentals=0
    )


def by_side(rank_ref, level, choose):
    rank = rank_ref[0]
    side = (rank >> level) & 1
    if level == 1:
        side ^= (rank >> 2) & 1
    for value in range(2):
        pl.when(side == value)(functools.partial(choose, value))


def load(*weights):
    count = len(weights)

    def kernel(*refs):
        sources, targets, done = refs[:count], refs[count : 2 * count], refs[-1]
        copies = [
            pltpu.make_async_copy(source, target, done.at[index])
            for index, (source, target) in enumerate(zip(sources, targets))
        ]
        for copy in copies:
            copy.start()
        for copy in copies:
            copy.wait()

    return pl.pallas_call(
        kernel,
        out_shape=tuple(jax.ShapeDtypeStruct(w.shape, w.dtype) for w in weights),
        in_specs=[HBM] * count,
        out_specs=(VMEM,) * count,
        scratch_shapes=[pltpu.SemaphoreType.DMA((count,))],
        compiler_params=params(LOAD_BYTES),
        cost_estimate=cost(0, 4 * sum(w.size for w in weights)),
        name="load",
    )(*weights)


def pieces(start, width):
    return [(at, at + PIECE) for at in range(start, start + width, PIECE)]


def forward(rank, tokens, w_in, w_out, start, width, after=()):
    parts = len(tokens)
    rows, features = tokens[0].shape[1:]
    total = parts * rows
    half = total // 2

    def kernel(rank_ref, *refs):
        token_refs = refs[:parts]
        wi_ref, wo_ref = refs[parts : parts + 2]
        keep_ref, send_ref = refs[-2:]

        def rows_of(which):
            return jnp.concatenate([ref[which] for ref in token_refs], axis=0)

        for low, high in pieces(start, width):
            at = slice(low - start, high - start)
            sums = (
                contract(rows_of(0), wi_ref[:, low:high], 1, 0),
                contract(rows_of(1), wo_ref[low:high, :], 1, 1),
            )

            def choose(core, at=at, sums=sums):
                for which, value in enumerate(sums):
                    halves = value[:half], value[half:]
                    keep_ref[which, :, at] = halves[core]
                    send_ref[which, :, at] = halves[1 - core].astype(BF16)

            by_side(rank_ref, 0, choose)

    return pl.pallas_call(
        kernel,
        grid=(1,),
        out_shape=(
            jax.ShapeDtypeStruct((2, half, width), F32),
            jax.ShapeDtypeStruct((2, half, width), BF16),
        ),
        in_specs=[SCALAR]
        + [whole(2, rows, features)] * parts
        + [VMEM, VMEM]
        + [ANY] * len(after),
        out_specs=(whole(2, half, width),) * 2,
        compiler_params=params(SMALL_BYTES),
        cost_estimate=cost(4 * total * features * width, 4 * features * width),
        name="forward",
    )(rank, *tokens, w_in, w_out, *after)


def halve(rank, keep, received, level, after=()):
    _, rows, width = keep.shape
    half = rows // 2

    def kernel(rank_ref, keep_ref, received_ref, *rest):
        next_ref, send_ref = rest[-2:]

        def choose(side):
            mine = slice(side * half, (side + 1) * half)
            other = slice((1 - side) * half, (2 - side) * half)
            next_ref[...] = keep_ref[:, mine] + received_ref[:, mine].astype(F32)
            send_ref[...] = (
                keep_ref[:, other] + received_ref[:, other].astype(F32)
            ).astype(BF16)

        by_side(rank_ref, level, choose)

    return pl.pallas_call(
        kernel,
        grid=(1,),
        out_shape=(
            jax.ShapeDtypeStruct((2, half, width), F32),
            jax.ShapeDtypeStruct((2, half, width), BF16),
        ),
        in_specs=[SCALAR] + [whole(2, rows, width)] * 2 + [ANY] * len(after),
        out_specs=(whole(2, half, width),) * 2,
        compiler_params=params(SMALL_BYTES),
        cost_estimate=cost(2 * rows * width, 12 * rows * width),
        name="halve",
    )(rank, keep, received, *after)


def activate(keep, received, after=()):
    def kernel(keep_ref, received_ref, *rest):
        out_ref = rest[-1]
        value, slope = gelu_parts(keep_ref[0] + received_ref[0].astype(F32))
        grad = keep_ref[1] + received_ref[1].astype(F32)
        out_ref[0] = value.astype(BF16)
        out_ref[1] = (grad * slope).astype(BF16)

    return pl.pallas_call(
        kernel,
        grid=(1,),
        out_shape=jax.ShapeDtypeStruct(keep.shape, BF16),
        in_specs=[whole(*keep.shape)] * 2 + [ANY] * len(after),
        out_specs=whole(*keep.shape),
        compiler_params=params(SMALL_BYTES),
        cost_estimate=cost(20 * keep.size, 8 * keep.size),
        name="activate",
    )(keep, received, *after)


def relay(array, after):
    def kernel(in_ref, *rest):
        rest[-1][...] = in_ref[...]

    return pl.pallas_call(
        kernel,
        grid=(1,),
        out_shape=jax.ShapeDtypeStruct(array.shape, array.dtype),
        in_specs=[whole(*array.shape)] + [ANY] * len(after),
        out_specs=whole(*array.shape),
        compiler_params=params(SMALL_BYTES),
        cost_estimate=cost(0, 4 * array.size),
        name="relay",
    )(array, *after)


def join(rank, own, received, level, after=()):
    _, half, width = own.shape

    def kernel(rank_ref, own_ref, received_ref, *rest):
        out_ref = rest[-1]

        def choose(side):
            out_ref[:, side * half : (side + 1) * half] = own_ref[...]
            out_ref[:, (1 - side) * half : (2 - side) * half] = received_ref[...]

        by_side(rank_ref, level, choose)

    return pl.pallas_call(
        kernel,
        grid=(1,),
        out_shape=jax.ShapeDtypeStruct((2, 2 * half, width), BF16),
        in_specs=[SCALAR] + [whole(2, half, width)] * 2 + [ANY] * len(after),
        out_specs=whole(2, 2 * half, width),
        compiler_params=params(SMALL_BYTES),
        cost_estimate=cost(0, 8 * own.size),
        name="join",
    )(rank, own, received, *after)


def join_line(rank, own, others, after=()):
    _, part, width = own.shape

    def kernel(rank_ref, own_ref, one_ref, two_ref, three_ref, *rest):
        out_ref = rest[-1]

        def outer(first):
            def inner(second):
                for flip, source in (
                    ((0, 0), own_ref),
                    ((1, 0), one_ref),
                    ((1, 1), two_ref),
                    ((0, 1), three_ref),
                ):
                    place = 2 * (first ^ flip[0]) + (second ^ flip[1])
                    out_ref[:, place * part : (place + 1) * part] = source[...]

            by_side(rank_ref, 2, inner)

        by_side(rank_ref, 1, outer)

    return pl.pallas_call(
        kernel,
        grid=(1,),
        out_shape=jax.ShapeDtypeStruct((2, 4 * part, width), BF16),
        in_specs=[SCALAR] + [whole(2, part, width)] * 4 + [ANY] * len(after),
        out_specs=whole(2, 4 * part, width),
        compiler_params=params(SMALL_BYTES),
        cost_estimate=cost(0, 16 * own.size),
        name="join_line",
    )(rank, own, *others, *after)


class Chunk:
    def __init__(self, rank, mp, keep, send, direct):
        self.rank, self.mp, self.levels = rank, mp, mp.bit_length() - 1
        self.keep, self.send, self.done = keep, send, 0
        self.direct = direct

    def advance(self, after=()):
        index, self.done = self.done, self.done + 1
        level = min(index, 2 * self.levels - 1 - index)
        if self.direct and index >= self.levels and level == 2:
            others = [exchange(self.send, "mp", self.mp, step) for step in (2, 4, 6)]
            self.done += 1
            self.send = join_line(self.rank, self.send, others, after)
            return self.send
        received = exchange(self.send, "mp", self.mp, partner_step(level))
        if index < self.levels - 1:
            self.keep, self.send = halve(
                self.rank, self.keep, received, level + 1, after
            )
        elif index == self.levels - 1:
            self.send = activate(self.keep, received, after)
        else:
            self.send = join(self.rank, self.send, received, level, after)
        return self.send

    def reach(self, done):
        while self.done < done:
            self.advance()


def input_grads(grads, w_in, carried, start):
    _, total, width = grads.shape
    features = w_in.shape[0]
    before = [] if carried is None else [carried]

    def kernel(grad_ref, wi_ref, *refs):
        value = refs[0][...] if before else 0.0
        for low, high in pieces(start, width):
            block = grad_ref[1, :, low - start : high - start]
            value = value + contract(block, wi_ref[:, low:high], 1, 1)
        refs[-1][...] = value

    return pl.pallas_call(
        kernel,
        grid=(1,),
        out_shape=jax.ShapeDtypeStruct((total, features), F32),
        in_specs=[whole(2, total, width), VMEM] + [whole(total, features)] * len(before),
        out_specs=whole(total, features),
        compiler_params=params(SMALL_BYTES),
        cost_estimate=cost(2 * total * features * width, 2 * features * width),
        name="input_grads",
    )(grads, w_in, *before)


def weight_grads(xt, gs, finals, factor):
    features, total = xt.shape
    width = finals[0].shape[2] // 2
    hidden = 2 * width * len(finals)

    def kernel(xt_ref, gs_ref, *refs):
        in_ref, out_ref = refs[-2:]
        step = pl.program_id(0)

        def work(final_ref):
            for low, high in pieces(0, width):
                act, grad = final_ref[0, :, low:high], final_ref[1, :, low:high]
                turned = act.astype(F32).T.astype(BF16)
                in_ref[:, low:high] = (contract(xt_ref[...], grad, 1, 0) * factor).astype(BF16)
                out_ref[low:high, :] = (contract(turned, gs_ref[...], 1, 0) * factor).astype(BF16)

        for index in range(len(finals)):
            pl.when((step >= 2 * index) & (step < 2 * index + 2))(functools.partial(work, refs[index]))

    def block(index):
        def place(i):
            return 0, 0, jnp.clip(i - 2 * index, 0, 1)

        return pl.BlockSpec((2, total, width), place)

    return pl.pallas_call(
        kernel,
        grid=(2 * len(finals),),
        out_shape=(
            jax.ShapeDtypeStruct((features, hidden), BF16),
            jax.ShapeDtypeStruct((hidden, features), BF16),
        ),
        in_specs=[whole(features, total), whole(total, features)]
        + [block(index) for index in range(len(finals))],
        out_specs=(
            pl.BlockSpec((features, width), lambda i: (0, i)),
            pl.BlockSpec((width, features), lambda i: (i, 0)),
        ),
        compiler_params=params(),
        cost_estimate=cost(4 * total * features * hidden, 4 * features * hidden),
        name="weight_grads",
    )(xt, gs, *finals)


def local(inputs, out_grads, w_in, w_out, dp, mp):
    hidden = w_in.shape[1]
    rows = inputs.shape[0]
    total = rows * dp
    factor = 1.0 / math.sqrt(total)
    rank = lax.axis_index("mp").astype(jnp.int32).reshape(1)
    width = hidden // CHUNKS
    starts = [index * width for index in range(CHUNKS)]

    own = jnp.stack([inputs, out_grads])
    parts = [own] + [exchange(own, "dp", dp, j) for j in range(1, dp)]

    w_in, w_out = load(w_in, w_out)

    chunks, after = [], []
    for start in starts:
        keep, send = forward(rank, parts, w_in, w_out, start, width, after)
        after = [send]
        for chunk in chunks[::-1]:
            after = [chunk.advance(after)]
        if chunks:
            after = [relay(send, after)]
            send = after[0]
        chunks.append(Chunk(rank, mp, keep, send, start == starts[-1]))

    steps = 2 * chunks[0].levels
    partial = None
    while any(chunk.done < steps for chunk in chunks):
        for chunk in chunks if chunks[0].done >= steps - 1 else chunks[::-1]:
            if chunk.done < steps:
                after = [chunk.advance(after)]
                if chunk.done == steps:
                    start = starts[chunks.index(chunk)]
                    partial = input_grads(chunk.send, w_in, partial, start)
                    after = [partial]
    finals = [chunk.send for chunk in chunks]

    in_total = partial[:rows]
    for j in range(1, dp):
        part = partial[j * rows : (j + 1) * rows].astype(BF16)
        in_total = in_total + exchange(part, "dp", dp, j).astype(F32)

    tokens = jnp.concatenate(parts, axis=1)
    unit = jnp.eye(total, dtype=BF16)
    xt = contract(tokens[0], unit, 0, 1).astype(BF16)
    return (in_total, *weight_grads(xt, tokens[1], finals, factor))


def solution(mesh):
    sizes = dict(mesh.shape)
    return jax.shard_map(
        functools.partial(local, dp=sizes["dp"], mp=sizes["mp"]),
        mesh=mesh,
        in_specs=(P("dp", "mp"), P("dp", "mp"), P("mp", "dp"), P("dp", "mp")),
        out_specs=(P("dp", "mp"), P("mp", "dp"), P("dp", "mp")),
        check_vma=False,
    )
```

```python
import functools
import math

import jax
import jax.numpy as jnp
from jax import lax
from jax.experimental import pallas as pl
from jax.experimental.pallas import tpu as pltpu
from jax.sharding import PartitionSpec as P

BF16 = jnp.bfloat16
F32 = jnp.float32
LOAD_BYTES = 24 * 1024 * 1024
CHUNKS = 2
PIECE = 384
VMEM_BYTES = 40 * 1024 * 1024
SMALL_BYTES = 16 * 1024 * 1024
SCALAR = pl.BlockSpec(memory_space=pltpu.SMEM)
ANY = pl.BlockSpec(memory_space=pl.ANY)
HBM = pl.BlockSpec(memory_space=pltpu.HBM)
VMEM = pl.BlockSpec(memory_space=pltpu.VMEM)


def gelu_parts(preact):
    cumul = 0.5 * (1.0 + jax.scipy.special.erf(preact * (1.0 / math.sqrt(2.0))))
    density = jnp.exp(-0.5 * preact * preact) * (1.0 / math.sqrt(2.0 * math.pi))
    return (preact * cumul, cumul + preact * density)


def contract(left, right, left_dim, right_dim):
    return lax.dot_general(
        left,
        right,
        (((left_dim,), (right_dim,)), ((), ())),
        preferred_element_type=F32,
    )


def exchange(array, axis, size, step):
    return lax.ppermute(array, axis, [(i, i ^ step) for i in range(size)])


def partner_step(level):
    return (1, 2, 6)[level] if level < 3 else 1 << level


def whole(*shape):
    return pl.BlockSpec(shape, lambda step: (0,) * len(shape))


def params(size=VMEM_BYTES):
    return pltpu.CompilerParams(vmem_limit_bytes=size)


def cost(flops, size):
    return pl.CostEstimate(
        flops=flops, bytes_accessed=size, transcendentals=0
    )


def by_side(rank_ref, level, choose):
    rank = rank_ref[0]
    side = (rank >> level) & 1
    if level == 1:
        side ^= (rank >> 2) & 1
    for value in range(2):
        pl.when(side == value)(functools.partial(choose, value))


def load(*weights):
    count = len(weights)

    def kernel(*refs):
        sources, targets, done = refs[:count], refs[count : 2 * count], refs[-1]
        copies = [
            pltpu.make_async_copy(source, target, done.at[index])
            for index, (source, target) in enumerate(zip(sources, targets))
        ]
        for copy in copies:
            copy.start()
        for copy in copies:
            copy.wait()

    return pl.pallas_call(
        kernel,
        out_shape=tuple(jax.ShapeDtypeStruct(w.shape, w.dtype) for w in weights),
        in_specs=[HBM] * count,
        out_specs=(VMEM,) * count,
        scratch_shapes=[pltpu.SemaphoreType.DMA((count,))],
        compiler_params=params(LOAD_BYTES),
        cost_estimate=cost(0, 4 * sum(w.size for w in weights)),
        name="load",
    )(*weights)


def pieces(start, width):
    return [(at, at + PIECE) for at in range(start, start + width, PIECE)]


def forward(rank, tokens, w_in, w_out, start, width, after=()):
    parts = len(tokens)
    rows, features = tokens[0].shape[1:]
    total = parts * rows
    half = total // 2

    def kernel(rank_ref, *refs):
        token_refs = refs[:parts]
        wi_ref, wo_ref = refs[parts : parts + 2]
        keep_ref, send_ref = refs[-2:]

        def rows_of(which):
            return jnp.concatenate([ref[which] for ref in token_refs], axis=0)

        for low, high in pieces(start, width):
            at = slice(low - start, high - start)
            sums = (
                contract(rows_of(0), wi_ref[:, low:high], 1, 0),
                contract(rows_of(1), wo_ref[low:high, :], 1, 1),
            )

            def choose(core, at=at, sums=sums):
                for which, value in enumerate(sums):
                    halves = value[:half], value[half:]
                    keep_ref[which, :, at] = halves[core]
                    send_ref[which, :, at] = halves[1 - core].astype(BF16)

            by_side(rank_ref, 0, choose)

    return pl.pallas_call(
        kernel,
        grid=(1,),
        out_shape=(
            jax.ShapeDtypeStruct((2, half, width), F32),
            jax.ShapeDtypeStruct((2, half, width), BF16),
        ),
        in_specs=[SCALAR]
        + [whole(2, rows, features)] * parts
        + [VMEM, VMEM]
        + [ANY] * len(after),
        out_specs=(whole(2, half, width),) * 2,
        compiler_params=params(SMALL_BYTES),
        cost_estimate=cost(4 * total * features * width, 4 * features * width),
        name="forward",
    )(rank, *tokens, w_in, w_out, *after)


def halve(rank, keep, received, level, after=()):
    _, rows, width = keep.shape
    half = rows // 2

    def kernel(rank_ref, keep_ref, received_ref, *rest):
        next_ref, send_ref = rest[-2:]

        def choose(side):
            mine = slice(side * half, (side + 1) * half)
            other = slice((1 - side) * half, (2 - side) * half)
            next_ref[...] = keep_ref[:, mine] + received_ref[:, mine].astype(F32)
            send_ref[...] = (
                keep_ref[:, other] + received_ref[:, other].astype(F32)
            ).astype(BF16)

        by_side(rank_ref, level, choose)

    return pl.pallas_call(
        kernel,
        grid=(1,),
        out_shape=(
            jax.ShapeDtypeStruct((2, half, width), F32),
            jax.ShapeDtypeStruct((2, half, width), BF16),
        ),
        in_specs=[SCALAR] + [whole(2, rows, width)] * 2 + [ANY] * len(after),
        out_specs=(whole(2, half, width),) * 2,
        compiler_params=params(SMALL_BYTES),
        cost_estimate=cost(2 * rows * width, 12 * rows * width),
        name="halve",
    )(rank, keep, received, *after)


def activate(keep, received, after=()):
    def kernel(keep_ref, received_ref, *rest):
        out_ref = rest[-1]
        value, slope = gelu_parts(keep_ref[0] + received_ref[0].astype(F32))
        grad = keep_ref[1] + received_ref[1].astype(F32)
        out_ref[0] = value.astype(BF16)
        out_ref[1] = (grad * slope).astype(BF16)

    return pl.pallas_call(
        kernel,
        grid=(1,),
        out_shape=jax.ShapeDtypeStruct(keep.shape, BF16),
        in_specs=[whole(*keep.shape)] * 2 + [ANY] * len(after),
        out_specs=whole(*keep.shape),
        compiler_params=params(SMALL_BYTES),
        cost_estimate=cost(20 * keep.size, 8 * keep.size),
        name="activate",
    )(keep, received, *after)


def relay(array, after):
    def kernel(in_ref, *rest):
        rest[-1][...] = in_ref[...]

    return pl.pallas_call(
        kernel,
        grid=(1,),
        out_shape=jax.ShapeDtypeStruct(array.shape, array.dtype),
        in_specs=[whole(*array.shape)] + [ANY] * len(after),
        out_specs=whole(*array.shape),
        compiler_params=params(SMALL_BYTES),
        cost_estimate=cost(0, 4 * array.size),
        name="relay",
    )(array, *after)


def join(rank, own, received, level, after=()):
    _, half, width = own.shape

    def kernel(rank_ref, own_ref, received_ref, *rest):
        out_ref = rest[-1]

        def choose(side):
            out_ref[:, side * half : (side + 1) * half] = own_ref[...]
            out_ref[:, (1 - side) * half : (2 - side) * half] = received_ref[...]

        by_side(rank_ref, level, choose)

    return pl.pallas_call(
        kernel,
        grid=(1,),
        out_shape=jax.ShapeDtypeStruct((2, 2 * half, width), BF16),
        in_specs=[SCALAR] + [whole(2, half, width)] * 2 + [ANY] * len(after),
        out_specs=whole(2, 2 * half, width),
        compiler_params=params(SMALL_BYTES),
        cost_estimate=cost(0, 8 * own.size),
        name="join",
    )(rank, own, received, *after)


class Chunk:
    def __init__(self, rank, mp, keep, send):
        self.rank, self.mp, self.levels = rank, mp, mp.bit_length() - 1
        self.keep, self.send, self.done = keep, send, 0

    def advance(self, after=()):
        index, self.done = self.done, self.done + 1
        level = min(index, 2 * self.levels - 1 - index)
        received = exchange(self.send, "mp", self.mp, partner_step(level))
        if index < self.levels - 1:
            self.keep, self.send = halve(
                self.rank, self.keep, received, level + 1, after
            )
        elif index == self.levels - 1:
            self.send = activate(self.keep, received, after)
        else:
            self.send = join(self.rank, self.send, received, level, after)
        return self.send

    def reach(self, done):
        while self.done < done:
            self.advance()


def input_grads(grads, w_in, carried, start):
    _, total, width = grads.shape
    features = w_in.shape[0]
    before = [] if carried is None else [carried]

    def kernel(grad_ref, wi_ref, *refs):
        value = refs[0][...] if before else 0.0
        for low, high in pieces(start, width):
            block = grad_ref[1, :, low - start : high - start]
            value = value + contract(block, wi_ref[:, low:high], 1, 1)
        refs[-1][...] = value

    return pl.pallas_call(
        kernel,
        grid=(1,),
        out_shape=jax.ShapeDtypeStruct((total, features), F32),
        in_specs=[whole(2, total, width), VMEM] + [whole(total, features)] * len(before),
        out_specs=whole(total, features),
        compiler_params=params(SMALL_BYTES),
        cost_estimate=cost(2 * total * features * width, 2 * features * width),
        name="input_grads",
    )(grads, w_in, *before)


def weight_grads(xt, gs, finals, factor):
    features, total = xt.shape
    width = finals[0].shape[2] // 2
    hidden = 2 * width * len(finals)

    def kernel(xt_ref, gs_ref, *refs):
        in_ref, out_ref = refs[-2:]
        step = pl.program_id(0)

        def work(final_ref):
            for low, high in pieces(0, width):
                act, grad = final_ref[0, :, low:high], final_ref[1, :, low:high]
                turned = act.astype(F32).T.astype(BF16)
                in_ref[:, low:high] = (contract(xt_ref[...], grad, 1, 0) * factor).astype(BF16)
                out_ref[low:high, :] = (contract(turned, gs_ref[...], 1, 0) * factor).astype(BF16)

        for index in range(len(finals)):
            pl.when((step >= 2 * index) & (step < 2 * index + 2))(functools.partial(work, refs[index]))

    def block(index):
        def place(i):
            return 0, 0, jnp.clip(i - 2 * index, 0, 1)

        return pl.BlockSpec((2, total, width), place)

    return pl.pallas_call(
        kernel,
        grid=(2 * len(finals),),
        out_shape=(
            jax.ShapeDtypeStruct((features, hidden), BF16),
            jax.ShapeDtypeStruct((hidden, features), BF16),
        ),
        in_specs=[whole(features, total), whole(total, features)]
        + [block(index) for index in range(len(finals))],
        out_specs=(
            pl.BlockSpec((features, width), lambda i: (0, i)),
            pl.BlockSpec((width, features), lambda i: (i, 0)),
        ),
        compiler_params=params(),
        cost_estimate=cost(4 * total * features * hidden, 4 * features * hidden),
        name="weight_grads",
    )(xt, gs, *finals)


def local(inputs, out_grads, w_in, w_out, dp, mp):
    hidden = w_in.shape[1]
    rows = inputs.shape[0]
    total = rows * dp
    factor = 1.0 / math.sqrt(total)
    rank = lax.axis_index("mp").astype(jnp.int32).reshape(1)
    width = hidden // CHUNKS
    starts = [index * width for index in range(CHUNKS)]

    own = jnp.stack([inputs, out_grads])
    parts = [own] + [exchange(own, "dp", dp, j) for j in range(1, dp)]

    w_in, w_out = load(w_in, w_out)

    chunks, after = [], []
    for start in starts:
        keep, send = forward(rank, parts, w_in, w_out, start, width, after)
        after = [send]
        for chunk in chunks[::-1]:
            after = [chunk.advance(after)]
        if chunks:
            after = [relay(send, after)]
            send = after[0]
        chunks.append(Chunk(rank, mp, keep, send))

    steps = 2 * chunks[0].levels
    partial = None
    while chunks[-1].done < steps:
        for chunk in chunks[::-1]:
            if chunk.done < steps:
                after = [chunk.advance(after)]
                if chunk.done == steps:
                    start = starts[chunks.index(chunk)]
                    partial = input_grads(chunk.send, w_in, partial, start)
                    after = [partial]
    finals = [chunk.send for chunk in chunks]

    in_total = partial[:rows]
    for j in range(1, dp):
        part = partial[j * rows : (j + 1) * rows].astype(BF16)
        in_total = in_total + exchange(part, "dp", dp, j).astype(F32)

    tokens = jnp.concatenate(parts, axis=1)
    unit = jnp.eye(total, dtype=BF16)
    xt = contract(tokens[0], unit, 0, 1).astype(BF16)
    return (in_total, *weight_grads(xt, tokens[1], finals, factor))


def solution(mesh):
    sizes = dict(mesh.shape)
    return jax.shard_map(
        functools.partial(local, dp=sizes["dp"], mp=sizes["mp"]),
        mesh=mesh,
        in_specs=(P("dp", "mp"), P("dp", "mp"), P("mp", "dp"), P("dp", "mp")),
        out_specs=(P("dp", "mp"), P("mp", "dp"), P("dp", "mp")),
        check_vma=False,
    )
```
